32 devices in a mesh: ctx: 4 (over y, x), head: 8 (over z, core).
Axes of the slice: x: 2, y: 2, z: 4, core: 2. Of those that a mesh axis runs over, the one named last changes fastest.
Arguments:
- latent: bfloat16 [1024, 576], P('ctx'), may hold values from -6 to 6
- queries: bfloat16 [1024, 24576], P('ctx', 'head'), may hold values from -300 to 300
- up_weight: bfloat16 [512, 32768], P(None, 'head'), may hold values from -0.25 to 0.25
- out_grad: bfloat16 [1024, 16384], P('ctx', 'head'), may hold values from -6 to 6
- logratio: float32 [1024], P('ctx'), may hold values from -1.5 to 1.5
- student_logprob: float32 [1024], P('ctx'), may hold values from -4 to -0.05
- teacher_logprob: float32 [1024], P('ctx'), may hold values from -4 to -0.05
- group_order: int32 [8], replicated, may hold values from 0 to 7, each once
Outputs:
- attn_output: bfloat16 [1024, 16384], P('ctx', 'head')
- query_grad: bfloat16 [1024, 24576], P('ctx', 'head')
- latent_grad: float32 [1024, 576], P(('ctx', 'head'))
- weight_grad: float32 [512, 32768], P('ctx', 'head')
The draws below stay inside these ranges and needn't reach their ends.
Inputs may be any that keep to these rules, and one draw needn't show every extreme that they name: Row r of the sequence arrays stands at position group_order[r // 128] * 128 + r % 128 of the rollout.
All inputs are finite; a program needn't handle non-finite values.
Results may differ from the reference program's by a relative error of at most 0.035.
Values may be sent and summed in bfloat16 or wider, within the bound.
A program may use at most 64 MiB of HBM per device.

```python
import jax
import jax.numpy as jnp
from jax import lax

H = 128
NOPE = 128
VDIM = 128
KV_RANK = 512
TOK_DEV = 256
LATENT = 576
QK = 192
SEQ = 1024
GROUP = 128
GROUPS = 8
N_CTX = 4


def latent_base(key):
    return jnp.clip(jax.random.normal(key, (SEQ, LATENT), jnp.float32), -6.0, 6.0)


def draw_latent(key, part):
    base = latent_base(key)
    return base.astype(jnp.bfloat16)


def draw_queries(key, part):
    key = jax.random.fold_in(key, 7)
    value_matrix = jnp.clip(jax.random.normal(key, (SEQ, H, QK), jnp.float32), -6.0, 6.0)
    value_matrix = jnp.clip(value_matrix, -300.0, 300.0)
    return value_matrix.reshape(SEQ, H * QK).astype(jnp.bfloat16)


def block_levels(rng, dims, cuts, smallest, top_value):
    factor_of = 1.0
    for position, blocks in cuts:
        draws = jax.random.uniform(jax.random.fold_in(jax.random.fold_in(rng, 6), position), (blocks,), jnp.float32, smallest / len(cuts), top_value / len(cuts))
        factor_of = factor_of * jnp.repeat(jnp.exp(draws), dims[position] // blocks).reshape((-1,) + (1,) * (len(dims) - 1 - position))
    return factor_of


def gaussian(stream_key, shape, scale, reach, split=(), held_as=jnp.bfloat16):
    result = jax.random.normal(stream_key, shape, jnp.float32) * scale
    if len(split) > 0:
        result = block_levels(stream_key, shape, split, -0.22, 0.18) * result
    return jnp.clip(result, min=-reach, max=reach).astype(held_as)


def setup_inputs(seed: int = 0) -> dict:
    keys = jax.random.split(jax.random.key(seed), 9)
    latent = draw_latent(jax.random.fold_in(keys[8], 71), 0)
    queries = draw_queries(jax.random.fold_in(keys[8], 71), 0)
    up_weight = gaussian(keys[2], (KV_RANK, H * (NOPE + VDIM)), KV_RANK ** -0.5, 0.25, ((1, 8),))
    out_grad = gaussian(keys[3], (SEQ, H * VDIM), 1.0, 6.0, ((0, 4), (1, 8)))
    logratio = gaussian(keys[4], (SEQ,), 0.3, 1.5, ((0, 4),), jnp.float32)
    student_logprob = jnp.clip(-4.0 + 3.95 * jax.random.uniform(keys[5], (SEQ,), jnp.float32) ** block_levels(keys[5], (SEQ,), ((0, 4),), -0.2, 0.2), -4.0, -0.05)
    teacher_logprob = jnp.clip(-4.0 + 3.95 * jax.random.uniform(keys[6], (SEQ,), jnp.float32) ** block_levels(keys[6], (SEQ,), ((0, 4),), -0.2, 0.2), -4.0, -0.05)
    group_order = jax.random.permutation(keys[7], GROUPS).astype(jnp.int32)
    return dict(latent=latent, queries=queries, up_weight=up_weight, out_grad=out_grad, logratio=logratio, student_logprob=student_logprob, teacher_logprob=teacher_logprob, group_order=group_order)


def positions_of(group_order, row_count, group_len):
    row_index = jnp.arange(row_count, dtype=jnp.int32)
    group_slot = row_index // group_len
    onehot = group_slot[:, None] == jnp.arange(group_order.shape[0], dtype=jnp.int32)[None, :]
    starts = jnp.sum(jnp.where(onehot, group_order[None, :], 0), axis=1).astype(jnp.int32)
    return starts * group_len + row_index % group_len


def token_weight(logratio, student_logprob, teacher_logprob):
    return jnp.clip(jnp.exp(logratio), 0.8, 1.25) * (teacher_logprob - student_logprob)


def head_block(head_query, head_grad, head_weight, latent, visible, tok_weight):
    logit_scale = QK ** -0.5
    latent_main = latent[:, :KV_RANK]
    key_value = jnp.dot(latent_main, head_weight, preferred_element_type=jnp.float32).astype(jnp.bfloat16)
    key_matrix = jnp.concatenate([key_value[:, :NOPE], latent[:, KV_RANK:]], axis=1).astype(jnp.float32)
    value_matrix = key_value[:, NOPE:].astype(jnp.float32)
    complete_query = head_query.astype(jnp.float32)
    score_matrix = jnp.einsum("jse,ne->jsn", complete_query, key_matrix) * logit_scale
    score_matrix = jnp.where(visible, score_matrix, -jnp.inf)
    row_max = jnp.max(score_matrix, axis=-1, keepdims=True)
    numerator = jnp.exp(score_matrix - row_max)
    attn_prob = numerator / jnp.sum(numerator, axis=-1, keepdims=True)
    probability_lowered = attn_prob.astype(jnp.bfloat16).astype(jnp.float32)
    attention_result = jnp.einsum("gfl,lh->gfh", probability_lowered, value_matrix)
    output_gradient = (tok_weight[..., None] * head_grad.astype(jnp.float32)).astype(jnp.bfloat16).astype(jnp.float32)
    probability_gradient = jnp.einsum("jse,ne->jsn", output_gradient, value_matrix)
    row_delta = jnp.sum(output_gradient * attention_result, axis=-1, keepdims=True)
    score_gradient = (attn_prob * (probability_gradient - row_delta) * logit_scale).astype(jnp.bfloat16).astype(jnp.float32)
    query_gradient = jnp.einsum("gfl,lh->gfh", score_gradient, key_matrix)
    key_gradient = jnp.einsum("uai,uaw->uiw", score_gradient, complete_query)
    value_gradient = jnp.einsum("uai,uaw->uiw", probability_lowered, output_gradient)
    grad_kv = jnp.concatenate([key_gradient[..., :NOPE], value_gradient], axis=-1).astype(jnp.bfloat16).astype(jnp.float32)
    grad_main = jnp.einsum("bkc,rc->kr", grad_kv, head_weight.astype(jnp.float32))
    grad_rope = jnp.sum(key_gradient[..., NOPE:], axis=0)
    grad_weight = jnp.einsum("kr,bkc->rc", latent_main.astype(jnp.float32), grad_kv)
    return attention_result.astype(jnp.bfloat16), query_gradient.astype(jnp.bfloat16), jnp.concatenate([grad_main, grad_rope], axis=1), grad_weight


def reference(latent, queries, up_weight, out_grad, logratio, student_logprob, teacher_logprob, group_order):
    positions = positions_of(group_order, SEQ, GROUP)
    visible = (positions[None, :] <= positions[:, None]).reshape(N_CTX, TOK_DEV, SEQ)
    tok_weight = token_weight(logratio, student_logprob, teacher_logprob).reshape(N_CTX, TOK_DEV)
    q_heads = queries.reshape(N_CTX, TOK_DEV, H, QK).transpose(2, 0, 1, 3)
    g_heads = out_grad.reshape(N_CTX, TOK_DEV, H, VDIM).transpose(2, 0, 1, 3)
    w_heads = up_weight.reshape(KV_RANK, H, NOPE + VDIM).transpose(1, 0, 2)

    def head_step(running, sliced):
        head_query, head_grad, head_weight = sliced
        attention_result, query_gradient, grad_latent, grad_weight = head_block(head_query, head_grad, head_weight, latent, visible, tok_weight)
        return running + grad_latent, (attention_result, query_gradient, grad_weight)

    start_value = jnp.zeros((SEQ, LATENT), jnp.float32)
    latent_grad, stacked = lax.scan(head_step, start_value, (q_heads, g_heads, w_heads))
    attn_output = stacked[0].transpose(1, 2, 0, 3).reshape(SEQ, H * VDIM)
    query_grad = stacked[1].transpose(1, 2, 0, 3).reshape(SEQ, H * QK)
    weight_grad = stacked[2].transpose(1, 0, 2).reshape(KV_RANK, H * (NOPE + VDIM))
    return attn_output, query_grad, latent_grad, weight_grad
```

```python
import functools

import jax
import jax.numpy as jnp
from jax import lax
from jax.experimental import pallas as pl
from jax.experimental.pallas import tpu as pltpu
from jax.sharding import PartitionSpec as P

NOPE = 128
VDIM = 128
KV_RANK = 512
QK = 192
ROPE = QK - NOPE
GROUP = 128
HIDDEN = -1e30


def dot(a, b):
    return jnp.dot(a, b, preferred_element_type=jnp.float32)


def dot_last(a, b):
    return lax.dot_general(a, b, (((1,), (1,)), ((), ())), preferred_element_type=jnp.float32)


def fill_bias(order_ref, bias, rows, n_slots):
    own = lax.axis_index("ctx") * (rows // GROUP)
    query_pos = jnp.concatenate(
        [
            order_ref[own + s] * GROUP + lax.broadcasted_iota(jnp.int32, (GROUP, GROUP), 1)
            for s in range(rows // GROUP)
        ],
        axis=1,
    )

    def slot(s, carry):
        key_pos = order_ref[s] * GROUP + lax.broadcasted_iota(jnp.int32, (GROUP, rows), 0)
        start = pl.multiple_of(s * GROUP, GROUP)
        bias[pl.ds(start, GROUP), :] = jnp.where(key_pos <= query_pos, 0.0, HIDDEN)
        return carry

    lax.fori_loop(0, n_slots, slot, 0)


def head_pair(pair, rope, q_ref, kv, dout, attn_ref, qg_ref, rope_acc, bias):
    scale = QK**-0.5
    q_at = pl.multiple_of(pair * (2 * QK), 2 * QK)
    o_at = pl.multiple_of(pair * (2 * VDIM), 2 * VDIM)
    query_pair = q_ref[:, pl.ds(q_at, 2 * QK)]
    query_grads = []
    rope_sum = None
    for j in range(2):
        kv_at = pl.multiple_of(pair * 512 + j * 256, 256)
        v_at = pl.multiple_of(pair * 256 + j * VDIM, VDIM)
        key = jnp.concatenate([kv[:, pl.ds(kv_at, NOPE)], rope], axis=1)
        value = kv[:, pl.ds(kv_at + NOPE, VDIM)]
        query = query_pair[:, j * QK : (j + 1) * QK]
        grad = dout[:, pl.ds(v_at, VDIM)]
        score = dot_last(key, query) + bias[...]
        top = jnp.max(score, axis=0, keepdims=True)
        weight = jnp.exp((score - top) * scale)
        prob = weight * (1.0 / jnp.sum(weight, axis=0, keepdims=True))
        prob_low = prob.astype(jnp.bfloat16)
        out_t = dot(value.T, prob_low)
        delta = jnp.sum(grad.astype(jnp.float32).T * out_t, axis=0, keepdims=True)
        attn_ref[:, pl.ds(v_at, VDIM)] = out_t.T.astype(jnp.bfloat16)
        dprob = dot_last(value, grad)
        dscore = (prob * (dprob - delta) * scale).astype(jnp.bfloat16)
        query_grads.append(dot(key.T, dscore).T)
        dkey = dot(dscore, query)
        dvalue = dot(prob_low, grad)
        kv[:, pl.ds(kv_at, NOPE)] = dkey[:, :NOPE].astype(jnp.bfloat16)
        kv[:, pl.ds(kv_at + NOPE, VDIM)] = dvalue.astype(jnp.bfloat16)
        part = dkey[:, NOPE:]
        rope_sum = part if rope_sum is None else rope_sum + part
    qg_ref[:, pl.ds(q_at, 2 * QK)] = jnp.concatenate(query_grads, axis=1).astype(jnp.bfloat16)
    rope_acc[...] += rope_sum


def kernel(
    lat_ref, q_ref, w_ref, g_ref, lr_ref, sl_ref, tl_ref, order_ref,
    attn_ref, qg_ref, lt_ref, wt_ref,
    kv, dout, bias, lat_t, rope_acc,
):
    rows, keys = q_ref.shape[0], lat_ref.shape[0]
    n_pairs = q_ref.shape[1] // (2 * QK)
    fill_bias(order_ref, bias, rows, keys // GROUP)
    tok_weight = jnp.clip(jnp.exp(lr_ref[...]), 0.8, 1.25) * (tl_ref[...] - sl_ref[...])
    tok_weight = jnp.broadcast_to(tok_weight, (128, rows)).T
    lat_t[...] = lat_ref[:, :KV_RANK].T
    rope_acc[...] = jnp.zeros_like(rope_acc)

    def pair_step(pair, carry):
        at = pl.multiple_of(pair * 512, 512)
        o_at = pl.multiple_of(pair * 256, 256)
        two = jnp.concatenate([tok_weight, tok_weight], axis=1)
        dout[:, pl.ds(o_at, 256)] = (two * g_ref[:, pl.ds(o_at, 256)].astype(jnp.float32)).astype(
            jnp.bfloat16
        )
        kv[:, pl.ds(at, 512)] = dot(lat_ref[:, :KV_RANK], w_ref[:, pl.ds(at, 512)]).astype(
            jnp.bfloat16
        )
        head_pair(
            pair, lat_ref[:, KV_RANK:], q_ref, kv, dout, attn_ref, qg_ref, rope_acc, bias
        )
        wt_ref[:, pl.ds(at, 512)] = dot(lat_t[...], kv[:, pl.ds(at, 512)]).astype(jnp.bfloat16)
        return carry

    lax.fori_loop(0, n_pairs, pair_step, 0)

    def chunk(i, carry):
        at = pl.multiple_of(i * 256, 256)
        lt_ref[pl.ds(at, 256), :KV_RANK] = dot_last(kv[pl.ds(at, 256), :], w_ref[...]).astype(
            jnp.bfloat16
        )
        lt_ref[pl.ds(at, 256), KV_RANK:] = rope_acc[pl.ds(at, 256), :].astype(jnp.bfloat16)
        return carry

    lax.fori_loop(0, keys // 256, chunk, 0)


def local(
    latent, queries, up_weight, out_grad, logratio, student_logprob, teacher_logprob, group_order
):
    gathered = lax.all_gather(latent, "ctx", axis=0, tiled=True)
    rows, keys = latent.shape[0], gathered.shape[0]
    vmem = pl.BlockSpec(memory_space=pltpu.VMEM)
    smem = pl.BlockSpec(memory_space=pltpu.SMEM)
    bf16 = jnp.bfloat16
    attn, query_grad, latent_terms, weight_terms = pl.pallas_call(
        kernel,
        out_shape=(
            jax.ShapeDtypeStruct(out_grad.shape, bf16),
            jax.ShapeDtypeStruct(queries.shape, bf16),
            jax.ShapeDtypeStruct(gathered.shape, bf16),
            jax.ShapeDtypeStruct(up_weight.shape, bf16),
        ),
        in_specs=[vmem] * 7 + [smem],
        out_specs=[vmem] * 4,
        scratch_shapes=[
            pltpu.VMEM((keys, up_weight.shape[1]), bf16),
            pltpu.VMEM((rows, out_grad.shape[1]), bf16),
            pltpu.VMEM((keys, rows), jnp.float32),
            pltpu.VMEM((KV_RANK, keys), bf16),
            pltpu.VMEM((keys, ROPE), jnp.float32),
        ],
        compiler_params=pltpu.CompilerParams(vmem_limit_bytes=60 * 2**20),
    )(
        gathered,
        queries,
        up_weight,
        out_grad,
        logratio.reshape(1, rows),
        student_logprob.reshape(1, rows),
        teacher_logprob.reshape(1, rows),
        group_order,
    )
    latent_grad = lax.psum_scatter(latent_terms, ("ctx", "head"), scatter_dimension=0, tiled=True)
    weight_grad = lax.psum_scatter(weight_terms, "ctx", scatter_dimension=0, tiled=True)
    return (
        attn,
        query_grad,
        latent_grad.astype(jnp.float32),
        weight_grad.astype(jnp.float32),
    )


def solution(mesh):
    placed = (
        P("ctx", None),
        P("ctx", "head"),
        P(None, "head"),
        P("ctx", "head"),
        P("ctx"),
        P("ctx"),
        P("ctx"),
        P(),
    )
    return jax.shard_map(
        local,
        mesh=mesh,
        in_specs=placed,
        out_specs=(P("ctx", "head"), P("ctx", "head"), P(("ctx", "head"), None), P("ctx", "head")),
        check_vma=False,
    )
```

```python
import functools

import jax
import jax.numpy as jnp
from jax import lax
from jax.experimental import pallas as pl
from jax.experimental.pallas import tpu as pltpu
from jax.sharding import PartitionSpec as P

NOPE = 128
VDIM = 128
KV_RANK = 512
QK = 192
ROPE = QK - NOPE
GROUP = 128
HIDDEN = -1e30


def dot(a, b):
    return jnp.dot(a, b, preferred_element_type=jnp.float32)


def dot_last(a, b):
    return lax.dot_general(a, b, (((1,), (1,)), ((), ())), preferred_element_type=jnp.float32)


def fill_bias(order_ref, bias, rows, n_slots):
    own = lax.axis_index("ctx") * (rows // GROUP)
    query_pos = jnp.concatenate(
        [
            order_ref[own + s] * GROUP + lax.broadcasted_iota(jnp.int32, (GROUP, GROUP), 1)
            for s in range(rows // GROUP)
        ],
        axis=1,
    )

    def slot(s, carry):
        key_pos = order_ref[s] * GROUP + lax.broadcasted_iota(jnp.int32, (GROUP, rows), 0)
        start = pl.multiple_of(s * GROUP, GROUP)
        bias[pl.ds(start, GROUP), :] = jnp.where(key_pos <= query_pos, 0.0, HIDDEN)
        return carry

    lax.fori_loop(0, n_slots, slot, 0)


def head_pair(pair, rope, q_ref, kv, dout, attn_ref, qg_ref, rope_acc, bias):
    scale = QK**-0.5
    q_at = pl.multiple_of(pair * (2 * QK), 2 * QK)
    o_at = pl.multiple_of(pair * (2 * VDIM), 2 * VDIM)
    query_pair = q_ref[:, pl.ds(q_at, 2 * QK)]
    query_grads = []
    rope_sum = None
    for j in range(2):
        kv_at = pl.multiple_of(pair * 512 + j * 256, 256)
        v_at = pl.multiple_of(pair * 256 + j * VDIM, VDIM)
        key = jnp.concatenate([kv[:, pl.ds(kv_at, NOPE)], rope], axis=1)
        value = kv[:, pl.ds(kv_at + NOPE, VDIM)]
        query = query_pair[:, j * QK : (j + 1) * QK]
        grad = dout[:, pl.ds(v_at, VDIM)]
        score = dot_last(key, query) + bias[...]
        top = jnp.max(score, axis=0, keepdims=True)
        weight = jnp.exp((score - top) * scale)
        prob = weight * (1.0 / jnp.sum(weight, axis=0, keepdims=True))
        prob_low = prob.astype(jnp.bfloat16)
        out_t = dot(value.T, prob_low)
        delta = jnp.sum(grad.astype(jnp.float32).T * out_t, axis=0, keepdims=True)
        attn_ref[:, pl.ds(v_at, VDIM)] = out_t.T.astype(jnp.bfloat16)
        dprob = dot_last(value, grad)
        dscore = (prob * (dprob - delta) * scale).astype(jnp.bfloat16)
        query_grads.append(dot(key.T, dscore).T)
        dkey = dot(dscore, query)
        dvalue = dot(prob_low, grad)
        kv[:, pl.ds(kv_at, NOPE)] = dkey[:, :NOPE].astype(jnp.bfloat16)
        kv[:, pl.ds(kv_at + NOPE, VDIM)] = dvalue.astype(jnp.bfloat16)
        part = dkey[:, NOPE:]
        rope_sum = part if rope_sum is None else rope_sum + part
    qg_ref[:, pl.ds(q_at, 2 * QK)] = jnp.concatenate(query_grads, axis=1).astype(jnp.bfloat16)
    rope_acc[...] += rope_sum


def remote(src, dst, send_sem, recv_sem, ctx, head):
    return pltpu.make_async_remote_copy(
        src_ref=src,
        dst_ref=dst,
        send_sem=send_sem,
        recv_sem=recv_sem,
        device_id=(ctx, head),
        device_id_type=pl.DeviceIdType.MESH,
    )


def kernel(
    n_ctx, n_head,
    lat_ref, lr_ref, sl_ref, tl_ref, order_ref, q_hbm, w_hbm, g_hbm,
    attn_ref, qg_ref, lg_ref, wg_ref,
    lat, q_ref, w_ref, g_ref, kv, dout, bias, lat_t, rope_acc,
    wt, wt_in, terms, core_in, comb, ctx_in, zsum, z_in,
    load_sem, lat_send, lat_recv, fwd_send, fwd_recv, wt_send, wt_recv,
    core_send, core_recv, ctx_send, ctx_recv, z_send, z_recv,
):
    rows, keys = lat_ref.shape[0], lat.shape[0]
    n_pairs = q_ref.shape[1] // (2 * QK)
    n_z = n_head // 2
    half = rows // 2
    own_rows = KV_RANK // n_ctx
    f32, bf16 = jnp.float32, jnp.bfloat16
    me, head = lax.axis_index("ctx"), lax.axis_index("head")
    core, z = head % 2, head // 2
    partner = head + 1 - 2 * core

    loads = [
        pltpu.make_async_copy(src, dst, load_sem.at[i])
        for i, (src, dst) in enumerate(((g_hbm, g_ref), (w_hbm, w_ref), (q_hbm, q_ref)))
    ]
    for load in loads:
        load.start()

    def ctx_peer(d):
        return (me + d) % n_ctx

    def ctx_source(d):
        return (me + n_ctx - d) % n_ctx

    def z_peer(d):
        return (z + d) % n_z

    barrier = pltpu.get_barrier_semaphore()
    peers = [(ctx_peer(d), head) for d in range(1, n_ctx)]
    peers += [(me, z_peer(d) * 2 + core) for d in range(1, n_z)]
    peers += [(me, partner)]
    for peer in peers:
        pl.semaphore_signal(barrier, inc=1, device_id=peer, device_id_type=pl.DeviceIdType.MESH)
    pl.semaphore_wait(barrier, len(peers))

    def lat_rows(block, part):
        return lat.at[pl.ds(pl.multiple_of(block * rows + part * half, half), half), :]

    def lat_copy(d, to, block, part):
        return remote(
            lat_ref.at[pl.ds(pl.multiple_of(core * half, half), half), :],
            lat_rows(block, part), lat_send.at[d - 1], lat_recv.at[d - 1], to, head,
        )

    def fwd_copy(d, part):
        place = lat_rows(ctx_source(d), part)
        return remote(place, place, fwd_send.at[d - 1], fwd_recv.at[d - 1], me, partner)

    order = [2, 1, 3] if n_ctx == 4 else list(range(1, n_ctx))
    for d in order:
        lat_copy(d, ctx_peer(d), me, core).start()
    lat[pl.ds(pl.multiple_of(me * rows, rows), rows), :] = lat_ref[...]

    fill_bias(order_ref, bias, rows, keys // GROUP)
    tok_weight = jnp.clip(jnp.exp(lr_ref[...]), 0.8, 1.25) * (tl_ref[...] - sl_ref[...])
    tok_weight = jnp.broadcast_to(tok_weight, (128, rows)).T
    two = jnp.concatenate([tok_weight, tok_weight], axis=1)
    rope_acc[...] = jnp.zeros_like(rope_acc)
    loads[0].wait()

    def weigh(pair, carry):
        at = pl.ds(pl.multiple_of(pair * 256, 256), 256)
        dout[:, at] = (two * g_ref[:, at].astype(f32)).astype(bf16)
        return carry

    lax.fori_loop(0, n_pairs, weigh, 0)

    for d in order:
        lat_copy(d, ctx_peer(d), ctx_source(d), core).wait_recv()
        fwd_copy(d, core).start()
    for d in order:
        fwd_copy(d, 1 - core).wait_recv()
    lat_t[...] = lat[:, :KV_RANK].T
    loads[1].wait()
    loads[2].wait()

    def wt_copy(d, pair):
        to = ctx_peer(d)
        return remote(
            wt.at[pair, pl.ds(pl.multiple_of(to * own_rows, own_rows), own_rows), :],
            wt_in.at[d - 1, pair], wt_send.at[d - 1, pair], wt_recv.at[d - 1, pair], to, head,
        )

    def pair_step(pair, carry):
        at = pl.multiple_of(pair * 512, 512)
        kv[:, pl.ds(at, 512)] = dot(lat[:, :KV_RANK], w_ref[:, pl.ds(at, 512)]).astype(bf16)
        head_pair(pair, lat[:, KV_RANK:], q_ref, kv, dout, attn_ref, qg_ref, rope_acc, bias)
        wt[pair] = dot(lat_t[...], kv[:, pl.ds(at, 512)]).astype(bf16)
        for d in order:
            wt_copy(d, pair).start()
        return carry

    lax.fori_loop(0, n_pairs, pair_step, 0)

    def core_copy(block):
        return remote(
            terms.at[block, :, 1 - core], core_in.at[block],
            core_send.at[block], core_recv.at[block], me, partner,
        )

    def ctx_copy(d):
        return remote(
            comb.at[d], ctx_in.at[d - 1], ctx_send.at[d - 1], ctx_recv.at[d - 1], ctx_peer(d), head
        )

    def z_copy(d):
        return remote(
            zsum.at[z_peer(d)], z_in.at[d - 1], z_send.at[d - 1], z_recv.at[d - 1],
            me, z_peer(d) * 2 + core,
        )

    def merged(block):
        core_copy(block).wait_recv()
        return terms[block, :, core].astype(f32) + core_in[block].astype(f32)

    def chunk(i, carry):
        block = (me + 1 + i) % n_ctx
        at = pl.ds(pl.multiple_of(block * rows, rows), rows)
        main = dot_last(kv[at, :], w_ref[...])
        whole = jnp.concatenate([main, rope_acc[at, :]], axis=1).astype(bf16)
        terms[block] = whole.reshape(terms.shape[1:])
        core_copy(block).start()

        @pl.when(i > 0)
        def _():
            comb[i] = merged((me + i) % n_ctx).astype(bf16)
            ctx_copy(i).start()

        return carry

    lax.fori_loop(0, n_ctx, chunk, 0)
    total = merged(me)
    for d in order:
        ctx_copy(d).wait_recv()
        total += ctx_in[d - 1].astype(f32)
    zsum[...] = total.astype(bf16)
    for d in range(1, n_z):
        z_copy(d).start()

    def gather_weight(pair, carry):
        at = pl.ds(pl.multiple_of(pair * 512, 512), 512)
        mine = pl.ds(pl.multiple_of(me * own_rows, own_rows), own_rows)
        total = wt[pair, mine, :].astype(f32)
        for d in order:
            wt_copy(d, pair).wait_recv()
            total += wt_in[d - 1, pair].astype(f32)
        wg_ref[:, at] = total
        return carry

    lax.fori_loop(0, n_pairs, gather_weight, 0)

    final = zsum[z].astype(f32)
    for d in range(1, n_z):
        z_copy(d).wait_recv()
        final += z_in[d - 1].astype(f32)
    lg_ref[...] = final

    for d in order:
        lat_copy(d, ctx_peer(d), me, core).wait_send()
        fwd_copy(d, core).wait_send()
        ctx_copy(d).wait_send()
    for d in range(1, n_z):
        z_copy(d).wait_send()

    def drain_core(block, carry):
        core_copy(block).wait_send()
        return carry

    lax.fori_loop(0, n_ctx, drain_core, 0)

    def drain_weight(pair, carry):
        for d in order:
            wt_copy(d, pair).wait_send()
        return carry

    lax.fori_loop(0, n_pairs, drain_weight, 0)


def local(
    n_ctx, n_head,
    latent, queries, up_weight, out_grad, logratio, student_logprob, teacher_logprob, group_order
):
    rows, width = latent.shape
    keys = rows * n_ctx
    n_z, per = n_head // 2, rows // n_head
    n_pairs = queries.shape[1] // (2 * QK)
    own_rows = KV_RANK // n_ctx
    vmem = pl.BlockSpec(memory_space=pltpu.VMEM)
    smem = pl.BlockSpec(memory_space=pltpu.SMEM)
    anywhere = pl.BlockSpec(memory_space=pl.ANY)
    bf16, f32 = jnp.bfloat16, jnp.float32
    dma = pltpu.SemaphoreType.DMA
    shape = jax.ShapeDtypeStruct
    return pl.pallas_call(
        functools.partial(kernel, n_ctx, n_head),
        out_shape=(
            shape(out_grad.shape, bf16),
            shape(queries.shape, bf16),
            shape((per, width), f32),
            shape((own_rows, up_weight.shape[1]), f32),
        ),
        in_specs=[vmem] * 4 + [smem] + [anywhere] * 3,
        out_specs=[vmem] * 4,
        scratch_shapes=[
            pltpu.VMEM((keys, width), bf16),
            pltpu.VMEM(queries.shape, bf16),
            pltpu.VMEM(up_weight.shape, bf16),
            pltpu.VMEM(out_grad.shape, bf16),
            pltpu.VMEM((keys, up_weight.shape[1]), bf16),
            pltpu.VMEM(out_grad.shape, bf16),
            pltpu.VMEM((keys, rows), f32),
            pltpu.VMEM((KV_RANK, keys), bf16),
            pltpu.VMEM((keys, ROPE), f32),
            pltpu.VMEM((n_pairs, KV_RANK, 512), bf16),
            pltpu.VMEM((n_ctx - 1, n_pairs, own_rows, 512), bf16),
            pltpu.VMEM((n_ctx, n_z, 2, per, width), bf16),
            pltpu.VMEM((n_ctx, n_z, per, width), bf16),
            pltpu.VMEM((n_ctx, n_z, per, width), bf16),
            pltpu.VMEM((n_ctx - 1, n_z, per, width), bf16),
            pltpu.VMEM((n_z, per, width), bf16),
            pltpu.VMEM((n_z - 1, per, width), bf16),
            dma((3,)),
            dma((n_ctx - 1,)),
            dma((n_ctx - 1,)),
            dma((n_ctx - 1,)),
            dma((n_ctx - 1,)),
            dma((n_ctx - 1, n_pairs)),
            dma((n_ctx - 1, n_pairs)),
            dma((n_ctx,)),
            dma((n_ctx,)),
            dma((n_ctx - 1,)),
            dma((n_ctx - 1,)),
            dma((n_z - 1,)),
            dma((n_z - 1,)),
        ],
        compiler_params=pltpu.CompilerParams(
            vmem_limit_bytes=60 * 2**20, collective_id=0, has_side_effects=True
        ),
    )(
        latent,
        logratio.reshape(1, rows),
        student_logprob.reshape(1, rows),
        teacher_logprob.reshape(1, rows),
        group_order,
        queries,
        up_weight,
        out_grad,
    )


def solution(mesh):
    placed = (
        P("ctx", None),
        P("ctx", "head"),
        P(None, "head"),
        P("ctx", "head"),
        P("ctx"),
        P("ctx"),
        P("ctx"),
        P(),
    )
    return jax.shard_map(
        functools.partial(local, mesh.shape["ctx"], mesh.shape["head"]),
        mesh=mesh,
        in_specs=placed,
        out_specs=(P("ctx", "head"), P("ctx", "head"), P(("ctx", "head"), None), P("ctx", "head")),
        check_vma=False,
    )
```

```python
import functools

import jax
import jax.numpy as jnp
from jax import lax
from jax.experimental import pallas as pl
from jax.experimental.pallas import tpu as pltpu
from jax.sharding import PartitionSpec as P

NOPE = 128
VDIM = 128
KV_RANK = 512
QK = 192
ROPE = QK - NOPE
GROUP = 128
HIDDEN = -1e30
LOG2_E = 1.4426950408889634


def dot(a, b):
    return jnp.dot(a, b, preferred_element_type=jnp.float32)


def dot_last(a, b):
    return lax.dot_general(a, b, (((1,), (1,)), ((), ())), preferred_element_type=jnp.float32)


def fill_bias(order_ref, bias, rows, n_slots):
    own = lax.axis_index("ctx") * (rows // GROUP)
    query_pos = jnp.concatenate(
        [
            order_ref[own + s] * GROUP + lax.broadcasted_iota(jnp.int32, (GROUP, GROUP), 1)
            for s in range(rows // GROUP)
        ],
        axis=1,
    )

    def slot(s, carry):
        key_pos = order_ref[s] * GROUP + lax.broadcasted_iota(jnp.int32, (GROUP, rows), 0)
        start = pl.multiple_of(s * GROUP, GROUP)
        bias[pl.ds(start, GROUP), :] = jnp.where(key_pos <= query_pos, 0.0, HIDDEN)
        return carry

    lax.fori_loop(0, n_slots, slot, 0)


def head_pair(pair, rope, q_ref, kv, dkv, dout, attn_ref, qg_ref, rope_acc, bias):
    scale = QK**-0.5
    q_at = pl.ds(pl.multiple_of(pair * (2 * QK), 2 * QK), 2 * QK)
    query_pair = q_ref[:, q_at]
    v_at = [pl.ds(pl.multiple_of(pair * 256 + j * VDIM, VDIM), VDIM) for j in range(2)]
    query = [query_pair[:, j * QK : (j + 1) * QK] for j in range(2)]
    grad = [dout[:, v_at[j]] for j in range(2)]

    def key(j):
        return jnp.concatenate([kv[:, j * 256 : j * 256 + NOPE], rope], axis=1)

    def value(j):
        return kv[:, j * 256 + NOPE : (j + 1) * 256]

    def softmax(score):
        top = jnp.max(score, axis=0, keepdims=True)
        weight = jnp.exp2((score - top) * (scale * LOG2_E))
        return weight * (1.0 / jnp.sum(weight, axis=0, keepdims=True))

    def value_side(j, prob_low):
        dprob = dot_last(value(j), grad[j])
        out_t = dot(value(j).T, prob_low)
        delta = jnp.sum(grad[j].astype(jnp.float32).T * out_t, axis=0, keepdims=True)
        attn_ref[:, v_at[j]] = out_t.T.astype(jnp.bfloat16)
        return dprob, delta

    def key_side(j, dscore, prob_low):
        dkey = dot(dscore, query[j])
        dvalue = dot(prob_low, grad[j])
        query_grad = dot(key(j).T, dscore).T
        at = pl.multiple_of(pair * 512 + j * 256, 256)
        dkv[:, pl.ds(at, NOPE)] = dkey[:, :NOPE].astype(jnp.bfloat16)
        dkv[:, pl.ds(at + NOPE, VDIM)] = dvalue.astype(jnp.bfloat16)
        return dkey[:, NOPE:], query_grad

    score = [dot_last(key(j), query[j]) + bias[...] for j in range(2)]
    prob, low, dprob, delta = [], [], [], []
    for j in range(2):
        prob.append(softmax(score[j]))
        low.append(prob[j].astype(jnp.bfloat16))
        grads, rest = value_side(j, low[j])
        dprob.append(grads)
        delta.append(rest)
    rope_grads, query_grads = [], []
    for j in range(2):
        dscore = (prob[j] * (dprob[j] - delta[j]) * scale).astype(jnp.bfloat16)
        rope_grad, query_grad = key_side(j, dscore, low[j])
        rope_grads.append(rope_grad)
        query_grads.append(query_grad)
    qg_ref[:, q_at] = jnp.concatenate(query_grads, axis=1).astype(jnp.bfloat16)
    rope_acc[...] += rope_grads[0] + rope_grads[1]


def remote(src, dst, send_sem, recv_sem, ctx, head):
    return pltpu.make_async_remote_copy(
        src_ref=src,
        dst_ref=dst,
        send_sem=send_sem,
        recv_sem=recv_sem,
        device_id=(ctx, head),
        device_id_type=pl.DeviceIdType.MESH,
    )


def kernel(
    n_ctx, n_head,
    lat_ref, lr_ref, sl_ref, tl_ref, order_ref, q_hbm, w_hbm, g_hbm,
    attn_ref, qg_ref, lg_ref, wg_ref,
    lat, q_ref, w_ref, g_ref, kv, dkv, dout, bias, lat_t, rope_acc,
    wt, a_in, a_sum, a_in2, b_in, b_sum, b_in2, terms, core_in, comb, ctx_in, zsum, z_in,
    load_sem, lat_send, lat_recv, fwd_send, fwd_recv, wt_send, wt_recv,
    core_send, core_recv, ctx_send, ctx_recv, z_send, z_recv,
):
    rows, keys = lat_ref.shape[1], lat.shape[0]
    n_pairs = q_ref.shape[1] // (2 * QK)
    n_z = n_head // 2
    n_minor = n_ctx // 2
    half = rows // 2
    f32, bf16 = jnp.float32, jnp.bfloat16
    me, head = lax.axis_index("ctx"), lax.axis_index("head")
    core, z = head % 2, head // 2
    partner = head + 1 - 2 * core

    loads = [
        pltpu.make_async_copy(src, dst, load_sem.at[i])
        for i, (src, dst) in enumerate(((g_hbm, g_ref), (w_hbm, w_ref), (q_hbm, q_ref)))
    ]
    for load in loads:
        load.start()

    def ctx_peer(d):
        return (me + d) % n_ctx

    def ctx_source(d):
        return (me + n_ctx - d) % n_ctx

    def z_peer(d):
        return (z + d) % n_z

    lat[pl.ds(pl.multiple_of(me * rows, rows), rows), :] = lat_ref[...].T
    barrier = pltpu.get_barrier_semaphore()
    peers = [(ctx_peer(d), head) for d in range(1, n_ctx)]
    peers += [(me, z_peer(d) * 2 + core) for d in range(1, n_z)]
    peers += [(me, partner)]
    for peer in peers:
        pl.semaphore_signal(barrier, inc=1, device_id=peer, device_id_type=pl.DeviceIdType.MESH)
    pl.semaphore_wait(barrier, len(peers))

    def lat_rows(block, part):
        return lat.at[pl.ds(pl.multiple_of(block * rows + part * half, half), half), :]

    def lat_copy(d, to, block, part):
        place = lat_rows(block, part)
        return remote(place, place, lat_send.at[d - 1], lat_recv.at[d - 1], to, head)

    def fwd_copy(d, part):
        place = lat_rows(ctx_source(d), part)
        return remote(place, place, fwd_send.at[d - 1], fwd_recv.at[d - 1], me, partner)

    order = [2, 1, 3] if n_ctx == 4 else list(range(1, n_ctx))
    for d in order:
        lat_copy(d, ctx_peer(d), me, core).start()

    fill_bias(order_ref, bias, rows, keys // GROUP)
    tok_weight = jnp.clip(jnp.exp(lr_ref[...]), 0.8, 1.25) * (tl_ref[...] - sl_ref[...])
    tok_weight = jnp.broadcast_to(tok_weight, (128, rows)).T
    two = jnp.concatenate([tok_weight, tok_weight], axis=1)
    rope_acc[...] = jnp.zeros_like(rope_acc)
    loads[0].wait()

    def weigh(pair, carry):
        at = pl.ds(pl.multiple_of(pair * 256, 256), 256)
        dout[:, at] = (two * g_ref[:, at].astype(f32)).astype(bf16)
        return carry

    lax.fori_loop(0, n_pairs, weigh, 0)

    for d in order:
        lat_copy(d, ctx_peer(d), ctx_source(d), core).wait_recv()
        fwd_copy(d, core).start()
    for d in order:
        fwd_copy(d, 1 - core).wait_recv()
    lat_t[...] = lat[:, :KV_RANK].T
    loads[1].wait()
    loads[2].wait()

    u, v = me // n_minor, me % n_minor
    u_peer = 1 - u

    def v_peer(d):
        return (v + d) % n_minor

    def minor_first(d, pair):
        return remote(
            wt.at[pair, 0, :, v_peer(d)], a_in.at[d - 1, pair],
            wt_send.at[d - 1, pair], wt_recv.at[d - 1, pair], u * n_minor + v_peer(d), head,
        )

    def major_first(pair):
        return remote(
            wt.at[pair, 1, u_peer], b_in.at[pair],
            wt_send.at[n_minor - 1, pair], wt_recv.at[n_minor - 1, pair],
            u_peer * n_minor + v, head,
        )

    def major_second(pair):
        return remote(
            a_sum.at[pair], a_in2.at[pair],
            wt_send.at[n_minor, pair], wt_recv.at[n_minor, pair], u_peer * n_minor + v, head,
        )

    def minor_second(d, pair):
        return remote(
            b_sum.at[d - 1, pair], b_in2.at[d - 1, pair],
            wt_send.at[n_minor + d, pair], wt_recv.at[n_minor + d, pair],
            u * n_minor + v_peer(d), head,
        )

    def pass_on(pair):
        total = wt[pair, 0, u_peer, v].astype(f32)
        for d in range(1, n_minor):
            minor_first(d, pair).wait_recv()
            total += a_in[d - 1, pair, u_peer].astype(f32)
        a_sum[pair] = total.astype(bf16)
        major_second(pair).start()
        major_first(pair).wait_recv()
        for d in range(1, n_minor):
            total = wt[pair, 1, u, v_peer(d)].astype(f32) + b_in[pair, v_peer(d)].astype(f32)
            b_sum[d - 1, pair] = total.astype(bf16)
            minor_second(d, pair).start()

    def pair_step(pair, carry):
        at = pl.ds(pl.multiple_of(pair * 512, 512), 512)
        kv[...] = dot(lat[:, :KV_RANK], w_ref[:, at]).astype(bf16)
        head_pair(
            pair, lat[:, KV_RANK:], q_ref, kv, dkv, dout, attn_ref, qg_ref, rope_acc, bias
        )
        term = dot(lat_t[...], dkv[:, at]).astype(bf16)
        for j in range(2):
            part = term[:, j * 256 : (j + 1) * 256]
            wt[pair, j] = part.reshape(wt.shape[2:])
        for d in range(1, n_minor):
            minor_first(d, pair).start()
        major_first(pair).start()

        @pl.when(pair > 0)
        def _():
            pass_on(pair - 1)

        return carry

    lax.fori_loop(0, n_pairs, pair_step, 0)

    def core_copy(block):
        return remote(
            terms.at[block, :, 1 - core], core_in.at[block],
            core_send.at[block], core_recv.at[block], me, partner,
        )

    def ctx_copy(d):
        return remote(
            comb.at[d], ctx_in.at[d - 1], ctx_send.at[d - 1], ctx_recv.at[d - 1], ctx_peer(d), head
        )

    def z_copy(d):
        return remote(
            zsum.at[z_peer(d)], z_in.at[d - 1], z_send.at[d - 1], z_recv.at[d - 1],
            me, z_peer(d) * 2 + core,
        )

    def merged(block):
        core_copy(block).wait_recv()
        return terms[block, :, core].astype(f32) + core_in[block].astype(f32)

    def chunk(i, carry):
        block = (me + 1 + i) % n_ctx
        at = pl.ds(pl.multiple_of(block * rows, rows), rows)
        main = dot_last(dkv[at, :], w_ref[...])
        whole = jnp.concatenate([main, rope_acc[at, :]], axis=1).astype(bf16)
        terms[block] = whole.reshape(terms.shape[1:])
        core_copy(block).start()

        @pl.when(i == 0)
        def _():
            pass_on(n_pairs - 1)

        @pl.when(i > 0)
        def _():
            comb[i] = merged((me + i) % n_ctx).astype(bf16)
            ctx_copy(i).start()

        return carry

    lax.fori_loop(0, n_ctx, chunk, 0)
    total = merged(me)
    for d in order:
        ctx_copy(d).wait_recv()
        total += ctx_in[d - 1].astype(f32)
    zsum[...] = total.astype(bf16)
    for d in range(1, n_z):
        z_copy(d).start()

    def gather_weight(pair, carry):
        major_second(pair).wait_recv()
        total = wt[pair, 0, u, v].astype(f32) + a_in2[pair].astype(f32)
        for d in range(1, n_minor):
            total += a_in[d - 1, pair, u].astype(f32)
        wg_ref[:, pl.ds(pl.multiple_of(pair * 512, 512), 256)] = total
        total = wt[pair, 1, u, v].astype(f32) + b_in[pair, v].astype(f32)
        for d in range(1, n_minor):
            minor_second(d, pair).wait_recv()
            total += b_in2[d - 1, pair].astype(f32)
        wg_ref[:, pl.ds(pl.multiple_of(pair * 512 + 256, 256), 256)] = total
        return carry

    lax.fori_loop(0, n_pairs, gather_weight, 0)

    final = zsum[z].astype(f32)
    for d in range(1, n_z):
        z_copy(d).wait_recv()
        final += z_in[d - 1].astype(f32)
    lg_ref[...] = final

    for d in order:
        lat_copy(d, ctx_peer(d), me, core).wait_send()
        fwd_copy(d, core).wait_send()
        ctx_copy(d).wait_send()
    for d in range(1, n_z):
        z_copy(d).wait_send()

    def drain_core(block, carry):
        core_copy(block).wait_send()
        return carry

    lax.fori_loop(0, n_ctx, drain_core, 0)

    def drain_weight(pair, carry):
        for d in range(1, n_minor):
            minor_first(d, pair).wait_send()
            minor_second(d, pair).wait_send()
        major_first(pair).wait_send()
        major_second(pair).wait_send()
        return carry

    lax.fori_loop(0, n_pairs, drain_weight, 0)


def local(
    n_ctx, n_head,
    latent, queries, up_weight, out_grad, logratio, student_logprob, teacher_logprob, group_order
):
    rows, width = latent.shape
    keys = rows * n_ctx
    n_z, per = n_head // 2, rows // n_head
    n_pairs = queries.shape[1] // (2 * QK)
    n_minor = n_ctx // 2
    own_rows = KV_RANK // n_ctx
    vmem = pl.BlockSpec(memory_space=pltpu.VMEM)
    smem = pl.BlockSpec(memory_space=pltpu.SMEM)
    anywhere = pl.BlockSpec(memory_space=pl.ANY)
    bf16, f32 = jnp.bfloat16, jnp.float32
    dma = pltpu.SemaphoreType.DMA
    shape = jax.ShapeDtypeStruct
    return pl.pallas_call(
        functools.partial(kernel, n_ctx, n_head),
        out_shape=(
            shape(out_grad.shape, bf16),
            shape(queries.shape, bf16),
            shape((per, width), f32),
            shape((own_rows, up_weight.shape[1]), f32),
        ),
        in_specs=[vmem] * 4 + [smem] + [anywhere] * 3,
        out_specs=[vmem] * 4,
        scratch_shapes=[
            pltpu.VMEM((keys, width), bf16),
            pltpu.VMEM(queries.shape, bf16),
            pltpu.VMEM(up_weight.shape, bf16),
            pltpu.VMEM(out_grad.shape, bf16),
            pltpu.VMEM((keys, 512), bf16),
            pltpu.VMEM((keys, up_weight.shape[1]), bf16),
            pltpu.VMEM(out_grad.shape, bf16),
            pltpu.VMEM((keys, rows), f32),
            pltpu.VMEM((KV_RANK, keys), bf16),
            pltpu.VMEM((keys, ROPE), f32),
            pltpu.VMEM((n_pairs, 2, 2, n_minor, own_rows, 256), bf16),
            pltpu.VMEM((n_minor - 1, n_pairs, 2, own_rows, 256), bf16),
            pltpu.VMEM((n_pairs, own_rows, 256), bf16),
            pltpu.VMEM((n_pairs, own_rows, 256), bf16),
            pltpu.VMEM((n_pairs, n_minor, own_rows, 256), bf16),
            pltpu.VMEM((n_minor - 1, n_pairs, own_rows, 256), bf16),
            pltpu.VMEM((n_minor - 1, n_pairs, own_rows, 256), bf16),
            pltpu.VMEM((n_ctx, n_z, 2, per, width), bf16),
            pltpu.VMEM((n_ctx, n_z, per, width), bf16),
            pltpu.VMEM((n_ctx, n_z, per, width), bf16),
            pltpu.VMEM((n_ctx - 1, n_z, per, width), bf16),
            pltpu.VMEM((n_z, per, width), bf16),
            pltpu.VMEM((n_z - 1, per, width), bf16),
            dma((3,)),
            dma((n_ctx - 1,)),
            dma((n_ctx - 1,)),
            dma((n_ctx - 1,)),
            dma((n_ctx - 1,)),
            dma((2 * n_minor, n_pairs)),
            dma((2 * n_minor, n_pairs)),
            dma((n_ctx,)),
            dma((n_ctx,)),
            dma((n_ctx - 1,)),
            dma((n_ctx - 1,)),
            dma((n_z - 1,)),
            dma((n_z - 1,)),
        ],
        compiler_params=pltpu.CompilerParams(
            vmem_limit_bytes=60 * 2**20, collective_id=0, has_side_effects=True
        ),
    )(
        latent.T,
        logratio.reshape(1, rows),
        student_logprob.reshape(1, rows),
        teacher_logprob.reshape(1, rows),
        group_order,
        queries,
        up_weight,
        out_grad,
    )


def solution(mesh):
    placed = (
        P("ctx", None),
        P("ctx", "head"),
        P(None, "head"),
        P("ctx", "head"),
        P("ctx"),
        P("ctx"),
        P("ctx"),
        P(),
    )
    return jax.shard_map(
        functools.partial(local, mesh.shape["ctx"], mesh.shape["head"]),
        mesh=mesh,
        in_specs=placed,
        out_specs=(P("ctx", "head"), P("ctx", "head"), P(("ctx", "head"), None), P("ctx", "head")),
        check_vma=False,
    )
```

```python
import functools

import jax
import jax.numpy as jnp
from jax import lax
from jax.experimental import pallas as pl
from jax.experimental.pallas import tpu as pltpu
from jax.sharding import PartitionSpec as P

NOPE = 128
VDIM = 128
KV_RANK = 512
QK = 192
ROPE = QK - NOPE
GROUP = 128
HIDDEN = -1e30
LOG2_E = 1.4426950408889634


def dot(a, b):
    return jnp.dot(a, b, preferred_element_type=jnp.float32)


def dot_last(a, b):
    return lax.dot_general(a, b, (((1,), (1,)), ((), ())), preferred_element_type=jnp.float32)


def fill_bias(order_ref, bias, rows, n_slots):
    own = lax.axis_index("ctx") * (rows // GROUP)
    query_pos = jnp.concatenate(
        [
            order_ref[own + s] * GROUP + lax.broadcasted_iota(jnp.int32, (GROUP, GROUP), 1)
            for s in range(rows // GROUP)
        ],
        axis=1,
    )

    def slot(s, carry):
        key_pos = order_ref[s] * GROUP + lax.broadcasted_iota(jnp.int32, (GROUP, rows), 0)
        start = pl.multiple_of(s * GROUP, GROUP)
        bias[pl.ds(start, GROUP), :] = jnp.where(key_pos <= query_pos, 0.0, HIDDEN)
        return carry

    lax.fori_loop(0, n_slots, slot, 0)


def head_pair(pair, rope, q_ref, kv, dkv, dout, attn_ref, qg_ref, rope_acc, bias):
    scale = QK**-0.5
    q_at = pl.ds(pl.multiple_of(pair * (2 * QK), 2 * QK), 2 * QK)
    query_pair = q_ref[:, q_at]
    v_at = [pl.ds(pl.multiple_of(pair * 256 + j * VDIM, VDIM), VDIM) for j in range(2)]
    query = [query_pair[:, j * QK : (j + 1) * QK] for j in range(2)]
    grad = [dout[:, v_at[j]] for j in range(2)]

    def key(j):
        at = pl.ds(pl.multiple_of(pair * 512 + j * 256, 256), NOPE)
        return jnp.concatenate([kv[:, at], rope], axis=1)

    def value(j):
        return kv[:, pl.ds(pl.multiple_of(pair * 512 + j * 256 + NOPE, VDIM), VDIM)]

    def softmax(score):
        top = jnp.max(score, axis=0, keepdims=True)
        weight = jnp.exp2((score - top) * (scale * LOG2_E))
        return weight * (1.0 / jnp.sum(weight, axis=0, keepdims=True))

    def value_side(j, prob_low):
        dprob = dot_last(value(j), grad[j])
        out_t = dot(value(j).T, prob_low)
        delta = jnp.sum(grad[j].astype(jnp.float32).T * out_t, axis=0, keepdims=True)
        attn_ref[:, v_at[j]] = out_t.T.astype(jnp.bfloat16)
        return dprob, delta

    def key_side(j, dscore, prob_low):
        dkey = dot(dscore, query[j])
        dvalue = dot(prob_low, grad[j])
        query_grad = dot(key(j).T, dscore).T
        at = pl.multiple_of(pair * 512 + j * 256, 256)
        dkv[:, pl.ds(at, NOPE)] = dkey[:, :NOPE].astype(jnp.bfloat16)
        dkv[:, pl.ds(at + NOPE, VDIM)] = dvalue.astype(jnp.bfloat16)
        return dkey[:, NOPE:], query_grad

    score = [dot_last(key(j), query[j]) + bias[...] for j in range(2)]
    prob, low, dprob, delta = [], [], [], []
    for j in range(2):
        prob.append(softmax(score[j]))
        low.append(prob[j].astype(jnp.bfloat16))
        grads, rest = value_side(j, low[j])
        dprob.append(grads)
        delta.append(rest)
    rope_grads, query_grads = [], []
    for j in range(2):
        dscore = (prob[j] * (dprob[j] - delta[j]) * scale).astype(jnp.bfloat16)
        rope_grad, query_grad = key_side(j, dscore, low[j])
        rope_grads.append(rope_grad)
        query_grads.append(query_grad)
    qg_ref[:, q_at] = jnp.concatenate(query_grads, axis=1).astype(jnp.bfloat16)
    rope_acc[...] += rope_grads[0] + rope_grads[1]


def remote(src, dst, send_sem, recv_sem, ctx, head):
    return pltpu.make_async_remote_copy(
        src_ref=src,
        dst_ref=dst,
        send_sem=send_sem,
        recv_sem=recv_sem,
        device_id=(ctx, head),
        device_id_type=pl.DeviceIdType.MESH,
    )


def kernel(
    n_ctx, n_head,
    lat_ref, lr_ref, sl_ref, tl_ref, order_ref, q_hbm, w_hbm, g_hbm,
    attn_ref, qg_ref, lg_ref, wg_ref,
    lat, q_ref, w_ref, g_ref, kv, dkv, dout, bias, lat_t, rope_acc,
    wt, a_in, a_sum, a_in2, b_in, b_sum, b_in2, terms, core_in, comb, ctx_in, zsum, z_in,
    load_sem, lat_send, lat_recv, fwd_send, fwd_recv, wt_send, wt_recv,
    core_send, core_recv, ctx_send, ctx_recv, z_send, z_recv,
):
    rows, keys = lat_ref.shape[1], lat.shape[0]
    n_pairs = q_ref.shape[1] // (2 * QK)
    n_z = n_head // 2
    n_minor = n_ctx // 2
    half = rows // 2
    f32, bf16 = jnp.float32, jnp.bfloat16
    me, head = lax.axis_index("ctx"), lax.axis_index("head")
    core, z = head % 2, head // 2
    partner = head + 1 - 2 * core

    loads = [
        pltpu.make_async_copy(src, dst, load_sem.at[i])
        for i, (src, dst) in enumerate(((g_hbm, g_ref), (w_hbm, w_ref), (q_hbm, q_ref)))
    ]
    for load in loads:
        load.start()

    def ctx_peer(d):
        return (me + d) % n_ctx

    def ctx_source(d):
        return (me + n_ctx - d) % n_ctx

    def z_peer(d):
        return (z + d) % n_z

    lat[pl.ds(pl.multiple_of(me * rows, rows), rows), :] = lat_ref[...].T
    barrier = pltpu.get_barrier_semaphore()
    peers = [(ctx_peer(d), head) for d in range(1, n_ctx)]
    peers += [(me, z_peer(d) * 2 + core) for d in range(1, n_z)]
    peers += [(me, partner)]
    for peer in peers:
        pl.semaphore_signal(barrier, inc=1, device_id=peer, device_id_type=pl.DeviceIdType.MESH)
    pl.semaphore_wait(barrier, len(peers))

    def lat_rows(block, part):
        return lat.at[pl.ds(pl.multiple_of(block * rows + part * half, half), half), :]

    def lat_copy(d, to, block, part):
        place = lat_rows(block, part)
        return remote(place, place, lat_send.at[d - 1], lat_recv.at[d - 1], to, head)

    def fwd_copy(d, part):
        place = lat_rows(ctx_source(d), part)
        return remote(place, place, fwd_send.at[d - 1], fwd_recv.at[d - 1], me, partner)

    order = [2, 1, 3] if n_ctx == 4 else list(range(1, n_ctx))
    for d in order:
        lat_copy(d, ctx_peer(d), me, core).start()

    fill_bias(order_ref, bias, rows, keys // GROUP)
    tok_weight = jnp.clip(jnp.exp(lr_ref[...]), 0.8, 1.25) * (tl_ref[...] - sl_ref[...])
    tok_weight = jnp.broadcast_to(tok_weight, (128, rows)).T
    two = jnp.concatenate([tok_weight, tok_weight], axis=1)
    rope_acc[...] = jnp.zeros_like(rope_acc)
    loads[0].wait()

    def weigh(pair, carry):
        at = pl.ds(pl.multiple_of(pair * 256, 256), 256)
        dout[:, at] = (two * g_ref[:, at].astype(f32)).astype(bf16)
        return carry

    lax.fori_loop(0, n_pairs, weigh, 0)

    def up_project(block):
        at = pl.ds(pl.multiple_of(block * rows, rows), rows)
        lat_t[:, at] = lat[at, :KV_RANK].T

        def columns(pair, carry):
            cols = pl.ds(pl.multiple_of(pair * 512, 512), 512)
            kv[at, cols] = dot(lat[at, :KV_RANK], w_ref[:, cols]).astype(bf16)
            return carry

        lax.fori_loop(0, n_pairs, columns, 0)

    def arrive(d):
        lat_copy(d, ctx_peer(d), ctx_source(d), core).wait_recv()
        fwd_copy(d, core).start()

    def use(d):
        fwd_copy(d, 1 - core).wait_recv()
        up_project(ctx_source(d))

    loads[1].wait()
    up_project(me)
    arrive(order[0])
    use(order[0])
    for d in order[1:]:
        arrive(d)
    for d in order[1:]:
        use(d)
    loads[2].wait()

    u, v = me // n_minor, me % n_minor
    u_peer = 1 - u

    def v_peer(d):
        return (v + d) % n_minor

    def minor_first(d, pair):
        return remote(
            wt.at[pair, 0, :, v_peer(d)], a_in.at[d - 1, pair],
            wt_send.at[d - 1, pair], wt_recv.at[d - 1, pair], u * n_minor + v_peer(d), head,
        )

    def major_first(pair):
        return remote(
            wt.at[pair, 1, u_peer], b_in.at[pair],
            wt_send.at[n_minor - 1, pair], wt_recv.at[n_minor - 1, pair],
            u_peer * n_minor + v, head,
        )

    def major_second(pair):
        return remote(
            a_sum.at[pair], a_in2.at[pair],
            wt_send.at[n_minor, pair], wt_recv.at[n_minor, pair], u_peer * n_minor + v, head,
        )

    def minor_second(d, pair):
        return remote(
            b_sum.at[d - 1, pair], b_in2.at[d - 1, pair],
            wt_send.at[n_minor + d, pair], wt_recv.at[n_minor + d, pair],
            u * n_minor + v_peer(d), head,
        )

    def pass_on(pair):
        total = wt[pair, 0, u_peer, v].astype(f32)
        for d in range(1, n_minor):
            minor_first(d, pair).wait_recv()
            total += a_in[d - 1, pair, u_peer].astype(f32)
        a_sum[pair] = total.astype(bf16)
        major_second(pair).start()
        major_first(pair).wait_recv()
        for d in range(1, n_minor):
            total = wt[pair, 1, u, v_peer(d)].astype(f32) + b_in[pair, v_peer(d)].astype(f32)
            b_sum[d - 1, pair] = total.astype(bf16)
            minor_second(d, pair).start()

    def pair_step(pair, carry):
        at = pl.ds(pl.multiple_of(pair * 512, 512), 512)
        head_pair(
            pair, lat[:, KV_RANK:], q_ref, kv, dkv, dout, attn_ref, qg_ref, rope_acc, bias
        )
        term = dot(lat_t[...], dkv[:, at]).astype(bf16)
        for j in range(2):
            part = term[:, j * 256 : (j + 1) * 256]
            wt[pair, j] = part.reshape(wt.shape[2:])
        for d in range(1, n_minor):
            minor_first(d, pair).start()
        major_first(pair).start()

        @pl.when(pair > 0)
        def _():
            pass_on(pair - 1)

        return carry

    lax.fori_loop(0, n_pairs, pair_step, 0)

    def core_copy(block):
        return remote(
            terms.at[block, :, 1 - core], core_in.at[block],
            core_send.at[block], core_recv.at[block], me, partner,
        )

    def ctx_copy(d):
        return remote(
            comb.at[d], ctx_in.at[d - 1], ctx_send.at[d - 1], ctx_recv.at[d - 1], ctx_peer(d), head
        )

    def z_copy(d):
        return remote(
            zsum.at[z_peer(d)], z_in.at[d - 1], z_send.at[d - 1], z_recv.at[d - 1],
            me, z_peer(d) * 2 + core,
        )

    def merged(block):
        core_copy(block).wait_recv()
        return terms[block, :, core].astype(f32) + core_in[block].astype(f32)

    def chunk(i, carry):
        block = (me + 1 + i) % n_ctx
        at = pl.ds(pl.multiple_of(block * rows, rows), rows)
        main = dot_last(dkv[at, :], w_ref[...])
        whole = jnp.concatenate([main, rope_acc[at, :]], axis=1).astype(bf16)
        terms[block] = whole.reshape(terms.shape[1:])
        core_copy(block).start()

        @pl.when(i == 0)
        def _():
            pass_on(n_pairs - 1)

        @pl.when(i > 0)
        def _():
            comb[i] = merged((me + i) % n_ctx).astype(bf16)
            ctx_copy(i).start()

        return carry

    lax.fori_loop(0, n_ctx, chunk, 0)
    total = merged(me)
    for d in order:
        ctx_copy(d).wait_recv()
        total += ctx_in[d - 1].astype(f32)
    zsum[...] = total.astype(bf16)
    for d in range(1, n_z):
        z_copy(d).start()

    def gather_weight(pair, carry):
        major_second(pair).wait_recv()
        total = wt[pair, 0, u, v].astype(f32) + a_in2[pair].astype(f32)
        for d in range(1, n_minor):
            total += a_in[d - 1, pair, u].astype(f32)
        wg_ref[:, pl.ds(pl.multiple_of(pair * 512, 512), 256)] = total
        total = wt[pair, 1, u, v].astype(f32) + b_in[pair, v].astype(f32)
        for d in range(1, n_minor):
            minor_second(d, pair).wait_recv()
            total += b_in2[d - 1, pair].astype(f32)
        wg_ref[:, pl.ds(pl.multiple_of(pair * 512 + 256, 256), 256)] = total
        return carry

    lax.fori_loop(0, n_pairs, gather_weight, 0)

    final = zsum[z].astype(f32)
    for d in range(1, n_z):
        z_copy(d).wait_recv()
        final += z_in[d - 1].astype(f32)
    lg_ref[...] = final

    for d in order:
        lat_copy(d, ctx_peer(d), me, core).wait_send()
        fwd_copy(d, core).wait_send()
        ctx_copy(d).wait_send()
    for d in range(1, n_z):
        z_copy(d).wait_send()

    def drain_core(block, carry):
        core_copy(block).wait_send()
        return carry

    lax.fori_loop(0, n_ctx, drain_core, 0)

    def drain_weight(pair, carry):
        for d in range(1, n_minor):
            minor_first(d, pair).wait_send()
            minor_second(d, pair).wait_send()
        major_first(pair).wait_send()
        major_second(pair).wait_send()
        return carry

    lax.fori_loop(0, n_pairs, drain_weight, 0)


def write_out(*refs):
    sem = refs[8]
    copies = [pltpu.make_async_copy(refs[i], refs[4 + i], sem.at[i]) for i in range(4)]
    for copy in copies:
        copy.start()
    for copy in copies:
        copy.wait()


def local(
    n_ctx, n_head,
    latent, queries, up_weight, out_grad, logratio, student_logprob, teacher_logprob, group_order
):
    rows, width = latent.shape
    keys = rows * n_ctx
    n_z, per = n_head // 2, rows // n_head
    n_pairs = queries.shape[1] // (2 * QK)
    n_minor = n_ctx // 2
    own_rows = KV_RANK // n_ctx
    vmem = pl.BlockSpec(memory_space=pltpu.VMEM)
    smem = pl.BlockSpec(memory_space=pltpu.SMEM)
    anywhere = pl.BlockSpec(memory_space=pl.ANY)
    bf16, f32 = jnp.bfloat16, jnp.float32
    dma = pltpu.SemaphoreType.DMA
    shape = jax.ShapeDtypeStruct
    results = pl.pallas_call(
        functools.partial(kernel, n_ctx, n_head),
        out_shape=(
            pltpu.VMEM(out_grad.shape, bf16),
            pltpu.VMEM(queries.shape, bf16),
            pltpu.VMEM((per, width), f32),
            pltpu.VMEM((own_rows, up_weight.shape[1]), f32),
        ),
        in_specs=[vmem] * 4 + [smem] + [anywhere] * 3,
        out_specs=[vmem] * 4,
        scratch_shapes=[
            pltpu.VMEM((keys, width), bf16),
            pltpu.VMEM(queries.shape, bf16),
            pltpu.VMEM(up_weight.shape, bf16),
            pltpu.VMEM(out_grad.shape, bf16),
            pltpu.VMEM((keys, up_weight.shape[1]), bf16),
            pltpu.VMEM((keys, up_weight.shape[1]), bf16),
            pltpu.VMEM(out_grad.shape, bf16),
            pltpu.VMEM((keys, rows), f32),
            pltpu.VMEM((KV_RANK, keys), bf16),
            pltpu.VMEM((keys, ROPE), f32),
            pltpu.VMEM((n_pairs, 2, 2, n_minor, own_rows, 256), bf16),
            pltpu.VMEM((n_minor - 1, n_pairs, 2, own_rows, 256), bf16),
            pltpu.VMEM((n_pairs, own_rows, 256), bf16),
            pltpu.VMEM((n_pairs, own_rows, 256), bf16),
            pltpu.VMEM((n_pairs, n_minor, own_rows, 256), bf16),
            pltpu.VMEM((n_minor - 1, n_pairs, own_rows, 256), bf16),
            pltpu.VMEM((n_minor - 1, n_pairs, own_rows, 256), bf16),
            pltpu.VMEM((n_ctx, n_z, 2, per, width), bf16),
            pltpu.VMEM((n_ctx, n_z, per, width), bf16),
            pltpu.VMEM((n_ctx, n_z, per, width), bf16),
            pltpu.VMEM((n_ctx - 1, n_z, per, width), bf16),
            pltpu.VMEM((n_z, per, width), bf16),
            pltpu.VMEM((n_z - 1, per, width), bf16),
            dma((3,)),
            dma((n_ctx - 1,)),
            dma((n_ctx - 1,)),
            dma((n_ctx - 1,)),
            dma((n_ctx - 1,)),
            dma((2 * n_minor, n_pairs)),
            dma((2 * n_minor, n_pairs)),
            dma((n_ctx,)),
            dma((n_ctx,)),
            dma((n_ctx - 1,)),
            dma((n_ctx - 1,)),
            dma((n_z - 1,)),
            dma((n_z - 1,)),
        ],
        compiler_params=pltpu.CompilerParams(
            vmem_limit_bytes=58 * 2**20, collective_id=0, has_side_effects=True
        ),
    )(
        latent.T,
        logratio.reshape(1, rows),
        student_logprob.reshape(1, rows),
        teacher_logprob.reshape(1, rows),
        group_order,
        queries,
        up_weight,
        out_grad,
    )
    return pl.pallas_call(
        write_out,
        out_shape=tuple(shape(result.shape, result.dtype) for result in results),
        in_specs=[anywhere] * 4,
        out_specs=[anywhere] * 4,
        scratch_shapes=[dma((4,))],
    )(*results)


def solution(mesh):
    placed = (
        P("ctx", None),
        P("ctx", "head"),
        P(None, "head"),
        P("ctx", "head"),
        P("ctx"),
        P("ctx"),
        P("ctx"),
        P(),
    )
    return jax.shard_map(
        functools.partial(local, mesh.shape["ctx"], mesh.shape["head"]),
        mesh=mesh,
        in_specs=placed,
        out_specs=(P("ctx", "head"), P("ctx", "head"), P(("ctx", "head"), None), P("ctx", "head")),
        check_vma=False,
    )
```

```python
import functools

import jax
import jax.numpy as jnp
from jax import lax
from jax.experimental import pallas as pl
from jax.experimental.pallas import tpu as pltpu
from jax.sharding import PartitionSpec as P

NOPE = 128
VDIM = 128
KV_RANK = 512
QK = 192
GROUP = 128
HIDDEN = -1e30
LOG2_E = 1.4426950408889634


def dot(a, b):
    return jnp.dot(a, b, preferred_element_type=jnp.float32)


def dot_last(a, b):
    return lax.dot_general(a, b, (((1,), (1,)), ((), ())), preferred_element_type=jnp.float32)


def fill_bias(order_ref, bias, rows, n_slots):
    own = lax.axis_index("ctx") * (rows // GROUP)
    query_pos = jnp.concatenate(
        [
            order_ref[own + s] * GROUP + lax.broadcasted_iota(jnp.int32, (GROUP, GROUP), 1)
            for s in range(rows // GROUP)
        ],
        axis=1,
    )

    def slot(s, carry):
        key_pos = order_ref[s] * GROUP + lax.broadcasted_iota(jnp.int32, (GROUP, rows), 0)
        start = pl.multiple_of(s * GROUP, GROUP)
        bias[pl.ds(start, GROUP), :] = jnp.where(key_pos <= query_pos, 0.0, HIDDEN)
        return carry

    lax.fori_loop(0, n_slots, slot, 0)


def head_pair(pair, rope, q_ref, kv, dkv, dout, attn_ref, qg_ref, acc, bias):
    scale = QK**-0.5
    q_at = pl.ds(pl.multiple_of(pair * (2 * QK), 2 * QK), 2 * QK)
    query_pair = q_ref[:, q_at]
    v_at = [pl.ds(pl.multiple_of(pair * 256 + j * VDIM, VDIM), VDIM) for j in range(2)]
    query = [query_pair[:, j * QK : (j + 1) * QK] for j in range(2)]
    grad = [dout[:, v_at[j]] for j in range(2)]

    def key(j):
        return jnp.concatenate([kv[:, j * 256 : j * 256 + NOPE], rope], axis=1)

    def value(j):
        return kv[:, j * 256 + NOPE : (j + 1) * 256]

    def softmax(score):
        top = jnp.max(score, axis=0, keepdims=True)
        weight = jnp.exp2((score - top) * (scale * LOG2_E))
        return weight * (1.0 / jnp.sum(weight, axis=0, keepdims=True))

    def value_side(j, prob_low):
        dprob = dot_last(value(j), grad[j])
        out_t = dot(value(j).T, prob_low)
        delta = jnp.sum(grad[j].astype(jnp.float32).T * out_t, axis=0, keepdims=True)
        attn_ref[:, v_at[j]] = out_t.T.astype(jnp.bfloat16)
        return dprob, delta

    def key_side(j, dscore, prob_low):
        dkey = dot(dscore, query[j])
        dvalue = dot(prob_low, grad[j])
        query_grad = dot(key(j).T, dscore).T
        dkv[:, j * 256 : j * 256 + NOPE] = dkey[:, :NOPE].astype(jnp.bfloat16)
        dkv[:, j * 256 + NOPE : (j + 1) * 256] = dvalue.astype(jnp.bfloat16)
        return dkey[:, NOPE:], query_grad

    score = [dot_last(key(j), query[j]) + bias[...] for j in range(2)]
    prob, low, dprob, delta = [], [], [], []
    for j in range(2):
        prob.append(softmax(score[j]))
        low.append(prob[j].astype(jnp.bfloat16))
        grads, rest = value_side(j, low[j])
        dprob.append(grads)
        delta.append(rest)
    rope_grads, query_grads = [], []
    for j in range(2):
        dscore = (prob[j] * (dprob[j] - delta[j]) * scale).astype(jnp.bfloat16)
        rope_grad, query_grad = key_side(j, dscore, low[j])
        rope_grads.append(rope_grad)
        query_grads.append(query_grad)
    qg_ref[:, q_at] = jnp.concatenate(query_grads, axis=1).astype(jnp.bfloat16)
    acc[:, KV_RANK:] += rope_grads[0] + rope_grads[1]


def remote(src, dst, send_sem, recv_sem, ctx, head):
    return pltpu.make_async_remote_copy(
        src_ref=src,
        dst_ref=dst,
        send_sem=send_sem,
        recv_sem=recv_sem,
        device_id=(ctx, head),
        device_id_type=pl.DeviceIdType.MESH,
    )


def kernel(
    n_ctx, n_head,
    lat_ref, lr_ref, sl_ref, tl_ref, order_ref, q_hbm, w_hbm, g_hbm,
    attn_ref, qg_ref, lg_ref, wg_ref,
    lat, q_ref, w_ref, g_ref, kv, dkv, dout, bias, lat_t, acc,
    wt, a_in, a_sum, a_in2, b_in, b_sum, b_in2, terms, core_in, comb, ctx_in, zsum, z_in,
    load_sem, lat_send, lat_recv, fwd_send, fwd_recv, wt_send, wt_recv,
    core_send, core_recv, ctx_send, ctx_recv, z_send, z_recv,
):
    rows, keys = lat_ref.shape[1], lat.shape[0]
    n_pairs = q_ref.shape[1] // (2 * QK)
    n_z = n_head // 2
    n_minor = n_ctx // 2
    half = rows // 2
    f32, bf16 = jnp.float32, jnp.bfloat16
    me, head = lax.axis_index("ctx"), lax.axis_index("head")
    core, z = head % 2, head // 2
    partner = head + 1 - 2 * core

    loads = [
        pltpu.make_async_copy(src, dst, load_sem.at[i])
        for i, (src, dst) in enumerate(((g_hbm, g_ref), (w_hbm, w_ref), (q_hbm, q_ref)))
    ]
    for load in loads:
        load.start()

    def ctx_peer(d):
        return (me + d) % n_ctx

    def ctx_source(d):
        return (me + n_ctx - d) % n_ctx

    def z_peer(d):
        return (z + d) % n_z

    lat[pl.ds(pl.multiple_of(me * rows, rows), rows), :] = lat_ref[...].T
    barrier = pltpu.get_barrier_semaphore()
    peers = [(ctx_peer(d), head) for d in range(1, n_ctx)]
    peers += [(me, z_peer(d) * 2 + core) for d in range(1, n_z)]
    peers += [(me, partner)]
    for peer in peers:
        pl.semaphore_signal(barrier, inc=1, device_id=peer, device_id_type=pl.DeviceIdType.MESH)
    pl.semaphore_wait(barrier, len(peers))

    def lat_rows(block, part):
        return lat.at[pl.ds(pl.multiple_of(block * rows + part * half, half), half), :]

    def lat_copy(d, to, block, part):
        place = lat_rows(block, part)
        return remote(place, place, lat_send.at[d - 1], lat_recv.at[d - 1], to, head)

    def fwd_copy(d, part):
        place = lat_rows(ctx_source(d), part)
        return remote(place, place, fwd_send.at[d - 1], fwd_recv.at[d - 1], me, partner)

    order = [2, 1, 3] if n_ctx == 4 else list(range(1, n_ctx))
    for d in order:
        lat_copy(d, ctx_peer(d), me, core).start()

    fill_bias(order_ref, bias, rows, keys // GROUP)
    tok_weight = jnp.clip(jnp.exp(lr_ref[...]), 0.8, 1.25) * (tl_ref[...] - sl_ref[...])
    tok_weight = jnp.broadcast_to(tok_weight, (128, rows)).T
    two = jnp.concatenate([tok_weight, tok_weight], axis=1)
    acc[...] = jnp.zeros_like(acc)
    loads[0].wait()

    def weigh(pair, carry):
        at = pl.ds(pl.multiple_of(pair * 256, 256), 256)
        dout[:, at] = (two * g_ref[:, at].astype(f32)).astype(bf16)
        return carry

    lax.fori_loop(0, n_pairs, weigh, 0)

    for d in order:
        lat_copy(d, ctx_peer(d), ctx_source(d), core).wait_recv()
        fwd_copy(d, core).start()
    for d in order:
        fwd_copy(d, 1 - core).wait_recv()
    lat_t[...] = lat[:, :KV_RANK].T
    loads[1].wait()
    loads[2].wait()

    u, v = me // n_minor, me % n_minor
    u_peer = 1 - u

    def v_peer(d):
        return (v + d) % n_minor

    def minor_first(d, pair):
        return remote(
            wt.at[pair, 0, :, v_peer(d)], a_in.at[d - 1, pair],
            wt_send.at[d - 1, pair], wt_recv.at[d - 1, pair], u * n_minor + v_peer(d), head,
        )

    def major_first(pair):
        return remote(
            wt.at[pair, 1, u_peer], b_in.at[pair],
            wt_send.at[n_minor - 1, pair], wt_recv.at[n_minor - 1, pair],
            u_peer * n_minor + v, head,
        )

    def major_second(pair):
        return remote(
            a_sum.at[pair], a_in2.at[pair],
            wt_send.at[n_minor, pair], wt_recv.at[n_minor, pair], u_peer * n_minor + v, head,
        )

    def minor_second(d, pair):
        return remote(
            b_sum.at[d - 1, pair], b_in2.at[d - 1, pair],
            wt_send.at[n_minor + d, pair], wt_recv.at[n_minor + d, pair],
            u * n_minor + v_peer(d), head,
        )

    def pass_on(pair):
        total = wt[pair, 0, u_peer, v].astype(f32)
        for d in range(1, n_minor):
            minor_first(d, pair).wait_recv()
            total += a_in[d - 1, pair, u_peer].astype(f32)
        a_sum[pair] = total.astype(bf16)
        major_second(pair).start()
        major_first(pair).wait_recv()
        for d in range(1, n_minor):
            total = wt[pair, 1, u, v_peer(d)].astype(f32) + b_in[pair, v_peer(d)].astype(f32)
            b_sum[d - 1, pair] = total.astype(bf16)
            minor_second(d, pair).start()

    def pair_step(pair, carry):
        at = pl.ds(pl.multiple_of(pair * 512, 512), 512)
        kv[...] = dot(lat[:, :KV_RANK], w_ref[:, at]).astype(bf16)
        head_pair(
            pair, lat[:, KV_RANK:], q_ref, kv, dkv, dout, attn_ref, qg_ref, acc, bias
        )
        acc[:, :KV_RANK] += dot_last(dkv[...], w_ref[:, at])
        term = dot(lat_t[...], dkv[...]).astype(bf16)
        for j in range(2):
            part = term[:, j * 256 : (j + 1) * 256]
            wt[pair, j] = part.reshape(wt.shape[2:])
        for d in range(1, n_minor):
            minor_first(d, pair).start()
        major_first(pair).start()

        @pl.when(pair > 1)
        def _():
            pass_on(pair - 2)

        return carry

    lax.fori_loop(0, n_pairs, pair_step, 0)

    def core_copy(block):
        return remote(
            terms.at[block, :, 1 - core], core_in.at[block],
            core_send.at[block], core_recv.at[block], me, partner,
        )

    def ctx_copy(d):
        return remote(
            comb.at[d], ctx_in.at[d - 1], ctx_send.at[d - 1], ctx_recv.at[d - 1], ctx_peer(d), head
        )

    def z_copy(d):
        return remote(
            zsum.at[z_peer(d)], z_in.at[d - 1], z_send.at[d - 1], z_recv.at[d - 1],
            me, z_peer(d) * 2 + core,
        )

    def merged(block):
        core_copy(block).wait_recv()
        return terms[block, :, core].astype(f32) + core_in[block].astype(f32)

    def to_partner(i, carry):
        block = (me + 1 + i) % n_ctx
        at = pl.ds(pl.multiple_of(block * rows, rows), rows)
        terms[block] = acc[at, :].astype(bf16).reshape(terms.shape[1:])
        core_copy(block).start()
        return carry

    def to_owner(d, carry):
        comb[d] = merged((me + d) % n_ctx).astype(bf16)
        ctx_copy(d).start()
        return carry

    lax.fori_loop(0, n_ctx, to_partner, 0)
    if n_pairs > 1:
        pass_on(n_pairs - 2)
    lax.fori_loop(1, n_ctx, to_owner, 0)
    pass_on(n_pairs - 1)
    total = merged(me)
    for d in order:
        ctx_copy(d).wait_recv()
        total += ctx_in[d - 1].astype(f32)
    zsum[...] = total.astype(bf16)
    for d in range(1, n_z):
        z_copy(d).start()

    def gather_weight(pair, carry):
        major_second(pair).wait_recv()
        total = wt[pair, 0, u, v].astype(f32) + a_in2[pair].astype(f32)
        for d in range(1, n_minor):
            total += a_in[d - 1, pair, u].astype(f32)
        wg_ref[:, pl.ds(pl.multiple_of(pair * 512, 512), 256)] = total
        total = wt[pair, 1, u, v].astype(f32) + b_in[pair, v].astype(f32)
        for d in range(1, n_minor):
            minor_second(d, pair).wait_recv()
            total += b_in2[d - 1, pair].astype(f32)
        wg_ref[:, pl.ds(pl.multiple_of(pair * 512 + 256, 256), 256)] = total
        return carry

    lax.fori_loop(0, n_pairs, gather_weight, 0)

    final = zsum[z].astype(f32)
    for d in range(1, n_z):
        z_copy(d).wait_recv()
        final += z_in[d - 1].astype(f32)
    lg_ref[...] = final

    for d in order:
        lat_copy(d, ctx_peer(d), me, core).wait_send()
        fwd_copy(d, core).wait_send()
        ctx_copy(d).wait_send()
    for d in range(1, n_z):
        z_copy(d).wait_send()

    def drain_core(block, carry):
        core_copy(block).wait_send()
        return carry

    lax.fori_loop(0, n_ctx, drain_core, 0)

    def drain_weight(pair, carry):
        for d in range(1, n_minor):
            minor_first(d, pair).wait_send()
            minor_second(d, pair).wait_send()
        major_first(pair).wait_send()
        major_second(pair).wait_send()
        return carry

    lax.fori_loop(0, n_pairs, drain_weight, 0)


def local(
    n_ctx, n_head,
    latent, queries, up_weight, out_grad, logratio, student_logprob, teacher_logprob, group_order
):
    rows, width = latent.shape
    keys = rows * n_ctx
    n_z, per = n_head // 2, rows // n_head
    n_pairs = queries.shape[1] // (2 * QK)
    n_minor = n_ctx // 2
    own_rows = KV_RANK // n_ctx
    vmem = pl.BlockSpec(memory_space=pltpu.VMEM)
    smem = pl.BlockSpec(memory_space=pltpu.SMEM)
    anywhere = pl.BlockSpec(memory_space=pl.ANY)
    bf16, f32 = jnp.bfloat16, jnp.float32
    dma = pltpu.SemaphoreType.DMA
    return pl.pallas_call(
        functools.partial(kernel, n_ctx, n_head),
        out_shape=(
            pltpu.VMEM(out_grad.shape, bf16),
            pltpu.VMEM(queries.shape, bf16),
            pltpu.VMEM((per, width), f32),
            pltpu.VMEM((own_rows, up_weight.shape[1]), f32),
        ),
        in_specs=[vmem] * 4 + [smem] + [anywhere] * 3,
        out_specs=[vmem] * 4,
        scratch_shapes=[
            pltpu.VMEM((keys, width), bf16),
            pltpu.VMEM(queries.shape, bf16),
            pltpu.VMEM(up_weight.shape, bf16),
            pltpu.VMEM(out_grad.shape, bf16),
            pltpu.VMEM((keys, 512), bf16),
            pltpu.VMEM((keys, 512), bf16),
            pltpu.VMEM(out_grad.shape, bf16),
            pltpu.VMEM((keys, rows), f32),
            pltpu.VMEM((KV_RANK, keys), bf16),
            pltpu.VMEM((keys, width), f32),
            pltpu.VMEM((n_pairs, 2, 2, n_minor, own_rows, 256), bf16),
            pltpu.VMEM((n_minor - 1, n_pairs, 2, own_rows, 256), bf16),
            pltpu.VMEM((n_pairs, own_rows, 256), bf16),
            pltpu.VMEM((n_pairs, own_rows, 256), bf16),
            pltpu.VMEM((n_pairs, n_minor, own_rows, 256), bf16),
            pltpu.VMEM((n_minor - 1, n_pairs, own_rows, 256), bf16),
            pltpu.VMEM((n_minor - 1, n_pairs, own_rows, 256), bf16),
            pltpu.VMEM((n_ctx, n_z, 2, per, width), bf16),
            pltpu.VMEM((n_ctx, n_z, per, width), bf16),
            pltpu.VMEM((n_ctx, n_z, per, width), bf16),
            pltpu.VMEM((n_ctx - 1, n_z, per, width), bf16),
            pltpu.VMEM((n_z, per, width), bf16),
            pltpu.VMEM((n_z - 1, per, width), bf16),
            dma((3,)),
            dma((n_ctx - 1,)),
            dma((n_ctx - 1,)),
            dma((n_ctx - 1,)),
            dma((n_ctx - 1,)),
            dma((2 * n_minor, n_pairs)),
            dma((2 * n_minor, n_pairs)),
            dma((n_ctx,)),
            dma((n_ctx,)),
            dma((n_ctx - 1,)),
            dma((n_ctx - 1,)),
            dma((n_z - 1,)),
            dma((n_z - 1,)),
        ],
        compiler_params=pltpu.CompilerParams(
            vmem_limit_bytes=58 * 2**20, collective_id=0, has_side_effects=True
        ),
    )(
        latent.T,
        logratio.reshape(1, rows),
        student_logprob.reshape(1, rows),
        teacher_logprob.reshape(1, rows),
        group_order,
        queries,
        up_weight,
        out_grad,
    )


def solution(mesh):
    placed = (
        P("ctx", None),
        P("ctx", "head"),
        P(None, "head"),
        P("ctx", "head"),
        P("ctx"),
        P("ctx"),
        P("ctx"),
        P(),
    )
    return jax.shard_map(
        functools.partial(local, mesh.shape["ctx"], mesh.shape["head"]),
        mesh=mesh,
        in_specs=placed,
        out_specs=(P("ctx", "head"), P("ctx", "head"), P(("ctx", "head"), None), P("ctx", "head")),
        check_vma=False,
    )
```

```python
import functools

import jax
import jax.numpy as jnp
from jax import lax
from jax.experimental import pallas as pl
from jax.experimental.pallas import tpu as pltpu
from jax.sharding import PartitionSpec as P

NOPE = 128
VDIM = 128
KV_RANK = 512
QK = 192
GROUP = 128
HIDDEN = -1e30
LOG2_E = 1.4426950408889634


def dot(a, b):
    return jnp.dot(a, b, preferred_element_type=jnp.float32)


def dot_last(a, b):
    return lax.dot_general(a, b, (((1,), (1,)), ((), ())), preferred_element_type=jnp.float32)


def fill_bias(order_ref, bias, rows, n_slots):
    own = lax.axis_index("ctx") * (rows // GROUP)
    query_pos = jnp.concatenate(
        [
            order_ref[own + s] * GROUP + lax.broadcasted_iota(jnp.int32, (GROUP, GROUP), 1)
            for s in range(rows // GROUP)
        ],
        axis=1,
    )

    def slot(s, carry):
        key_pos = order_ref[s] * GROUP + lax.broadcasted_iota(jnp.int32, (GROUP, rows), 0)
        start = pl.multiple_of(s * GROUP, GROUP)
        bias[pl.ds(start, GROUP), :] = jnp.where(key_pos <= query_pos, 0.0, HIDDEN)
        return carry

    lax.fori_loop(0, n_slots, slot, 0)


def head_pair(pair, rope, q_ref, kv, dkv, dout, attn_ref, qg_ref, acc, bias, beside):
    scale = QK**-0.5
    q_at = pl.ds(pl.multiple_of(pair * (2 * QK), 2 * QK), 2 * QK)
    query_pair = q_ref[:, q_at]
    v_at = [pl.ds(pl.multiple_of(pair * 256 + j * VDIM, VDIM), VDIM) for j in range(2)]
    query = [query_pair[:, j * QK : (j + 1) * QK] for j in range(2)]
    grad = [dout[:, v_at[j]] for j in range(2)]

    def key(j):
        return jnp.concatenate([kv[:, j * 256 : j * 256 + NOPE], rope], axis=1)

    def value(j):
        return kv[:, j * 256 + NOPE : (j + 1) * 256]

    def softmax(score):
        top = jnp.max(score, axis=0, keepdims=True)
        weight = jnp.exp2((score - top) * (scale * LOG2_E))
        return weight * (1.0 / jnp.sum(weight, axis=0, keepdims=True))

    def value_side(j, prob_low):
        dprob = dot_last(value(j), grad[j])
        out_t = dot(value(j).T, prob_low)
        delta = jnp.sum(grad[j].astype(jnp.float32).T * out_t, axis=0, keepdims=True)
        attn_ref[:, v_at[j]] = out_t.T.astype(jnp.bfloat16)
        return dprob, delta

    def key_side(j, dscore, prob_low):
        dkey = dot(dscore, query[j])
        dvalue = dot(prob_low, grad[j])
        query_grad = dot(key(j).T, dscore).T
        dkv[:, j * 256 : j * 256 + NOPE] = dkey[:, :NOPE].astype(jnp.bfloat16)
        dkv[:, j * 256 + NOPE : (j + 1) * 256] = dvalue.astype(jnp.bfloat16)
        return dkey[:, NOPE:], query_grad

    score = [dot_last(key(j), query[j]) + bias[...] for j in range(2)]
    beside()
    prob, low, dprob, delta = [], [], [], []
    for j in range(2):
        prob.append(softmax(score[j]))
        low.append(prob[j].astype(jnp.bfloat16))
        grads, rest = value_side(j, low[j])
        dprob.append(grads)
        delta.append(rest)
    rope_grads, query_grads = [], []
    for j in range(2):
        dscore = (prob[j] * (dprob[j] - delta[j]) * scale).astype(jnp.bfloat16)
        rope_grad, query_grad = key_side(j, dscore, low[j])
        rope_grads.append(rope_grad)
        query_grads.append(query_grad)
    qg_ref[:, q_at] = jnp.concatenate(query_grads, axis=1).astype(jnp.bfloat16)
    acc[:, KV_RANK:] += rope_grads[0] + rope_grads[1]


def remote(src, dst, send_sem, recv_sem, ctx, head):
    return pltpu.make_async_remote_copy(
        src_ref=src,
        dst_ref=dst,
        send_sem=send_sem,
        recv_sem=recv_sem,
        device_id=(ctx, head),
        device_id_type=pl.DeviceIdType.MESH,
    )


def kernel(
    n_ctx, n_head,
    lat_ref, lr_ref, sl_ref, tl_ref, order_ref, q_hbm, w_hbm, g_hbm,
    attn_ref, qg_ref, lg_ref, wg_ref,
    lat, q_ref, w_ref, g_ref, kv, dkv, dout, bias, lat_t, acc,
    wt, a_in, a_sum, a_in2, b_in, b_sum, b_in2, terms, core_in, comb, ctx_in, zsum, z_in,
    load_sem, lat_send, lat_recv, fwd_send, fwd_recv, wt_send, wt_recv,
    core_send, core_recv, ctx_send, ctx_recv, z_send, z_recv,
):
    rows, keys = lat_ref.shape[1], lat.shape[0]
    n_pairs = q_ref.shape[1] // (2 * QK)
    n_z = n_head // 2
    n_minor = n_ctx // 2
    half = rows // 2
    f32, bf16 = jnp.float32, jnp.bfloat16
    me, head = lax.axis_index("ctx"), lax.axis_index("head")
    core, z = head % 2, head // 2
    partner = head + 1 - 2 * core

    loads = [
        pltpu.make_async_copy(src, dst, load_sem.at[i])
        for i, (src, dst) in enumerate(((g_hbm, g_ref), (w_hbm, w_ref), (q_hbm, q_ref)))
    ]
    for load in loads:
        load.start()

    def ctx_peer(d):
        return (me + d) % n_ctx

    def ctx_source(d):
        return (me + n_ctx - d) % n_ctx

    def z_peer(d):
        return (z + d) % n_z

    lat[pl.ds(pl.multiple_of(me * rows, rows), rows), :] = lat_ref[...].T
    barrier = pltpu.get_barrier_semaphore()
    peers = [(ctx_peer(d), head) for d in range(1, n_ctx)]
    peers += [(me, z_peer(d) * 2 + core) for d in range(1, n_z)]
    peers += [(me, partner)]
    for peer in peers:
        pl.semaphore_signal(barrier, inc=1, device_id=peer, device_id_type=pl.DeviceIdType.MESH)
    pl.semaphore_wait(barrier, len(peers))

    def lat_rows(block, part):
        return lat.at[pl.ds(pl.multiple_of(block * rows + part * half, half), half), :]

    def lat_copy(d, to, block, part):
        place = lat_rows(block, part)
        return remote(place, place, lat_send.at[d - 1], lat_recv.at[d - 1], to, head)

    def fwd_copy(d, part):
        place = lat_rows(ctx_source(d), part)
        return remote(place, place, fwd_send.at[d - 1], fwd_recv.at[d - 1], me, partner)

    order = [2, 1, 3] if n_ctx == 4 else list(range(1, n_ctx))
    for d in order:
        lat_copy(d, ctx_peer(d), me, core).start()

    fill_bias(order_ref, bias, rows, keys // GROUP)
    tok_weight = jnp.clip(jnp.exp(lr_ref[...]), 0.8, 1.25) * (tl_ref[...] - sl_ref[...])
    tok_weight = jnp.broadcast_to(tok_weight, (128, rows)).T
    two = jnp.concatenate([tok_weight, tok_weight], axis=1)
    acc[...] = jnp.zeros_like(acc)
    loads[0].wait()

    def weigh(pair, carry):
        at = pl.ds(pl.multiple_of(pair * 256, 256), 256)
        dout[:, at] = (two * g_ref[:, at].astype(f32)).astype(bf16)
        return carry

    lax.fori_loop(0, n_pairs, weigh, 0)

    for d in order:
        lat_copy(d, ctx_peer(d), ctx_source(d), core).wait_recv()
        fwd_copy(d, core).start()
    for d in order:
        fwd_copy(d, 1 - core).wait_recv()
    lat_t[...] = lat[:, :KV_RANK].T
    loads[1].wait()
    loads[2].wait()

    u, v = me // n_minor, me % n_minor
    u_peer = 1 - u

    def v_peer(d):
        return (v + d) % n_minor

    def minor_first(d, pair):
        return remote(
            wt.at[pair, 0, :, v_peer(d)], a_in.at[d - 1, pair],
            wt_send.at[d - 1, pair], wt_recv.at[d - 1, pair], u * n_minor + v_peer(d), head,
        )

    def major_first(pair):
        return remote(
            wt.at[pair, 1, u_peer], b_in.at[pair],
            wt_send.at[n_minor - 1, pair], wt_recv.at[n_minor - 1, pair],
            u_peer * n_minor + v, head,
        )

    def major_second(pair):
        return remote(
            a_sum.at[pair], a_in2.at[pair],
            wt_send.at[n_minor, pair], wt_recv.at[n_minor, pair], u_peer * n_minor + v, head,
        )

    def minor_second(d, pair):
        return remote(
            b_sum.at[d - 1, pair], b_in2.at[d - 1, pair],
            wt_send.at[n_minor + d, pair], wt_recv.at[n_minor + d, pair],
            u * n_minor + v_peer(d), head,
        )

    def pass_on(pair):
        total = wt[pair, 0, u_peer, v].astype(f32)
        for d in range(1, n_minor):
            minor_first(d, pair).wait_recv()
            total += a_in[d - 1, pair, u_peer].astype(f32)
        a_sum[pair] = total.astype(bf16)
        major_second(pair).start()
        major_first(pair).wait_recv()
        for d in range(1, n_minor):
            total = wt[pair, 1, u, v_peer(d)].astype(f32) + b_in[pair, v_peer(d)].astype(f32)
            b_sum[d - 1, pair] = total.astype(bf16)
            minor_second(d, pair).start()

    def latent_terms(pair):
        at = pl.ds(pl.multiple_of(pair * 512, 512), 512)
        acc[:, :KV_RANK] += dot_last(dkv[...], w_ref[:, at])

    def weight_terms(pair):
        term = dot(lat_t[...], dkv[...]).astype(bf16)
        for j in range(2):
            part = term[:, j * 256 : (j + 1) * 256]
            wt[pair, j] = part.reshape(wt.shape[2:])

    def send_weight_terms(pair):
        for d in range(1, n_minor):
            minor_first(d, pair).start()
        major_first(pair).start()

    def pair_step(pair, carry):
        at = pl.ds(pl.multiple_of(pair * 512, 512), 512)
        before = (pair + n_pairs - 1) % n_pairs
        kv[...] = dot(lat[:, :KV_RANK], w_ref[:, at]).astype(bf16)

        def beside():
            latent_terms(before)
            weight_terms(before)

        head_pair(
            pair, lat[:, KV_RANK:], q_ref, kv, dkv, dout, attn_ref, qg_ref, acc, bias, beside
        )

        @pl.when(pair > 0)
        def _():
            send_weight_terms(pair - 1)

        @pl.when(pair > 1)
        def _():
            pass_on(pair - 2)

        return carry

    dkv[...] = jnp.zeros_like(dkv)
    lax.fori_loop(0, n_pairs, pair_step, 0)

    def core_copy(block):
        return remote(
            terms.at[block, :, 1 - core], core_in.at[block],
            core_send.at[block], core_recv.at[block], me, partner,
        )

    def ctx_copy(d):
        return remote(
            comb.at[d], ctx_in.at[d - 1], ctx_send.at[d - 1], ctx_recv.at[d - 1], ctx_peer(d), head
        )

    def z_copy(d):
        return remote(
            zsum.at[z_peer(d)], z_in.at[d - 1], z_send.at[d - 1], z_recv.at[d - 1],
            me, z_peer(d) * 2 + core,
        )

    def merged(block):
        core_copy(block).wait_recv()
        return terms[block, :, core].astype(f32) + core_in[block].astype(f32)

    def to_partner(i, carry):
        block = (me + 1 + i) % n_ctx
        at = pl.ds(pl.multiple_of(block * rows, rows), rows)
        terms[block] = acc[at, :].astype(bf16).reshape(terms.shape[1:])
        core_copy(block).start()
        return carry

    def to_owner(d, carry):
        comb[d] = merged((me + d) % n_ctx).astype(bf16)
        ctx_copy(d).start()
        return carry

    latent_terms(n_pairs - 1)
    lax.fori_loop(0, n_ctx, to_partner, 0)
    weight_terms(n_pairs - 1)
    send_weight_terms(n_pairs - 1)
    if n_pairs > 1:
        pass_on(n_pairs - 2)
    lax.fori_loop(1, n_ctx, to_owner, 0)
    pass_on(n_pairs - 1)
    total = merged(me)
    for d in order:
        ctx_copy(d).wait_recv()
        total += ctx_in[d - 1].astype(f32)
    zsum[...] = total.astype(bf16)
    for d in range(1, n_z):
        z_copy(d).start()

    def gather_weight(pair, carry):
        major_second(pair).wait_recv()
        total = wt[pair, 0, u, v].astype(f32) + a_in2[pair].astype(f32)
        for d in range(1, n_minor):
            total += a_in[d - 1, pair, u].astype(f32)
        wg_ref[:, pl.ds(pl.multiple_of(pair * 512, 512), 256)] = total
        total = wt[pair, 1, u, v].astype(f32) + b_in[pair, v].astype(f32)
        for d in range(1, n_minor):
            minor_second(d, pair).wait_recv()
            total += b_in2[d - 1, pair].astype(f32)
        wg_ref[:, pl.ds(pl.multiple_of(pair * 512 + 256, 256), 256)] = total
        return carry

    lax.fori_loop(0, n_pairs, gather_weight, 0)

    final = zsum[z].astype(f32)
    for d in range(1, n_z):
        z_copy(d).wait_recv()
        final += z_in[d - 1].astype(f32)
    lg_ref[...] = final

    for d in order:
        lat_copy(d, ctx_peer(d), me, core).wait_send()
        fwd_copy(d, core).wait_send()
        ctx_copy(d).wait_send()
    for d in range(1, n_z):
        z_copy(d).wait_send()

    def drain_core(block, carry):
        core_copy(block).wait_send()
        return carry

    lax.fori_loop(0, n_ctx, drain_core, 0)

    def drain_weight(pair, carry):
        for d in range(1, n_minor):
            minor_first(d, pair).wait_send()
            minor_second(d, pair).wait_send()
        major_first(pair).wait_send()
        major_second(pair).wait_send()
        return carry

    lax.fori_loop(0, n_pairs, drain_weight, 0)


def local(
    n_ctx, n_head,
    latent, queries, up_weight, out_grad, logratio, student_logprob, teacher_logprob, group_order
):
    rows, width = latent.shape
    keys = rows * n_ctx
    n_z, per = n_head // 2, rows // n_head
    n_pairs = queries.shape[1] // (2 * QK)
    n_minor = n_ctx // 2
    own_rows = KV_RANK // n_ctx
    vmem = pl.BlockSpec(memory_space=pltpu.VMEM)
    smem = pl.BlockSpec(memory_space=pltpu.SMEM)
    anywhere = pl.BlockSpec(memory_space=pl.ANY)
    bf16, f32 = jnp.bfloat16, jnp.float32
    dma = pltpu.SemaphoreType.DMA
    return pl.pallas_call(
        functools.partial(kernel, n_ctx, n_head),
        out_shape=(
            pltpu.VMEM(out_grad.shape, bf16),
            pltpu.VMEM(queries.shape, bf16),
            pltpu.VMEM((per, width), f32),
            pltpu.VMEM((own_rows, up_weight.shape[1]), f32),
        ),
        in_specs=[vmem] * 4 + [smem] + [anywhere] * 3,
        out_specs=[vmem] * 4,
        scratch_shapes=[
            pltpu.VMEM((keys, width), bf16),
            pltpu.VMEM(queries.shape, bf16),
            pltpu.VMEM(up_weight.shape, bf16),
            pltpu.VMEM(out_grad.shape, bf16),
            pltpu.VMEM((keys, 512), bf16),
            pltpu.VMEM((keys, 512), bf16),
            pltpu.VMEM(out_grad.shape, bf16),
            pltpu.VMEM((keys, rows), f32),
            pltpu.VMEM((KV_RANK, keys), bf16),
            pltpu.VMEM((keys, width), f32),
            pltpu.VMEM((n_pairs, 2, 2, n_minor, own_rows, 256), bf16),
            pltpu.VMEM((n_minor - 1, n_pairs, 2, own_rows, 256), bf16),
            pltpu.VMEM((n_pairs, own_rows, 256), bf16),
            pltpu.VMEM((n_pairs, own_rows, 256), bf16),
            pltpu.VMEM((n_pairs, n_minor, own_rows, 256), bf16),
            pltpu.VMEM((n_minor - 1, n_pairs, own_rows, 256), bf16),
            pltpu.VMEM((n_minor - 1, n_pairs, own_rows, 256), bf16),
            pltpu.VMEM((n_ctx, n_z, 2, per, width), bf16),
            pltpu.VMEM((n_ctx, n_z, per, width), bf16),
            pltpu.VMEM((n_ctx, n_z, per, width), bf16),
            pltpu.VMEM((n_ctx - 1, n_z, per, width), bf16),
            pltpu.VMEM((n_z, per, width), bf16),
            pltpu.VMEM((n_z - 1, per, width), bf16),
            dma((3,)),
            dma((n_ctx - 1,)),
            dma((n_ctx - 1,)),
            dma((n_ctx - 1,)),
            dma((n_ctx - 1,)),
            dma((2 * n_minor, n_pairs)),
            dma((2 * n_minor, n_pairs)),
            dma((n_ctx,)),
            dma((n_ctx,)),
            dma((n_ctx - 1,)),
            dma((n_ctx - 1,)),
            dma((n_z - 1,)),
            dma((n_z - 1,)),
        ],
        compiler_params=pltpu.CompilerParams(
            vmem_limit_bytes=58 * 2**20, collective_id=0, has_side_effects=True
        ),
    )(
        latent.T,
        logratio.reshape(1, rows),
        student_logprob.reshape(1, rows),
        teacher_logprob.reshape(1, rows),
        group_order,
        queries,
        up_weight,
        out_grad,
    )


def solution(mesh):
    placed = (
        P("ctx", None),
        P("ctx", "head"),
        P(None, "head"),
        P("ctx", "head"),
        P("ctx"),
        P("ctx"),
        P("ctx"),
        P(),
    )
    return jax.shard_map(
        functools.partial(local, mesh.shape["ctx"], mesh.shape["head"]),
        mesh=mesh,
        in_specs=placed,
        out_specs=(P("ctx", "head"), P("ctx", "head"), P(("ctx", "head"), None), P("ctx", "head")),
        check_vma=False,
    )
```
